128 devices in a mesh: ctx: 16 (over x, z), head: 8 (over y, core).
Axes of the slice: x: 4, y: 4, z: 4, core: 2. Of those that a mesh axis runs over, the one named last changes fastest.
Arguments:
- tokens: bfloat16 [16384, 7168], P(('ctx', 'head')), may hold values from -6 to 6
- routes: int32 [16384, 8], P(('ctx', 'head')), may hold values from 0 to 255, all different within a row; in each aligned block of 128 rows (0 to 127, 128 to 255, ...) at most 6 rows name the same one
- route_weight: float32 [16384, 8], P(('ctx', 'head')), may hold values from 0.2 to 2
- w_gate: bfloat16 [16, 7168, 1024], P('ctx', 'head'), may hold values from -0.0625 to 0.0625
- w_up: bfloat16 [16, 7168, 1024], P('ctx', 'head'), may hold values from -0.0625 to 0.0625
- w_down: bfloat16 [16, 1024, 7168], P('ctx', None, 'head'), may hold values from -0.1875 to 0.1875
- grad_out: bfloat16 [16384, 7168], P(('ctx', 'head')), may hold values from -6 to 6
Outputs:
- moe_out: bfloat16 [16384, 7168], P(('ctx', 'head'))
- grad_tokens: bfloat16 [16384, 7168], P(('ctx', 'head'))
- grad_route: float32 [16384, 8], P(('ctx', 'head'))
- grad_gate: bfloat16 [16, 7168, 1024], P('ctx', 'head')
- grad_up: bfloat16 [16, 7168, 1024], P('ctx', 'head')
- grad_down: bfloat16 [16, 1024, 7168], P('ctx', None, 'head')
The draws below stay inside these ranges and needn't reach their ends.
Inputs may be any that keep to these rules, and one draw needn't show every extreme that they name: `routes`: each row names 8 different experts. In each aligned block of 128 rows (the tokens of one device) no expert is named more than 6 times. Experts below 16 are the window's.
All inputs are finite; a program needn't handle non-finite values.
Results may differ from the reference program's by a relative error of at most 0.0057.
Values may be sent and summed in bfloat16 or wider, within the bound.
No kernel may reach another device: no remote copies, remote signals or barrier semaphores. Data moves between devices by JAX's collectives and lax.ppermute only.
A program may use at most 128 MiB of HBM per device.

```python
import math
import jax
import jax.numpy as jnp
import numpy as np
from jax import lax

D = 7168
FFE = 1024
ALL_EXP = 256
TOPK = 8
TOK_DEV = 128
EXPERTS = 16
CAP = 6
TOKENS = 16384


def levels(stream_key, extent, split, low, largest):
    def one(dim, blocks):
        heights = jax.random.uniform(jax.random.fold_in(jax.random.fold_in(stream_key, 6), dim), (blocks,), jnp.float32, low / len(split), largest / len(split))
        return jnp.repeat(jnp.exp(heights), extent[dim] // blocks).reshape((-1,) + (1,) * (len(extent) - dim - 1))

    level = one(*split[0])
    for cut in split[1:]:
        level = level * one(*cut)
    return level


def assign_block(stream_key, own, number, rows, number_of, top, limit, lean):
    sequence = jax.random.permutation(stream_key, number_of)
    crowded, ordinary = load_shares(number_of, rows * top, limit, lean, True), load_shares(number_of, rows * top, limit, lean, False)
    places = jnp.arange(number_of)

    def named(tallies, offset_by):
        used = int((tallies > 0).sum())
        fixed = max(1, used // 4)
        moved = fixed + (places - fixed + offset_by * (used - fixed)) % max(1, number_of - fixed)
        return jnp.zeros((number_of,), jnp.int32).at[sequence[jnp.where(places < fixed, places, moved)]].set(jnp.asarray(tallies, jnp.int32))

    tallies = jnp.where(number % 4 == 0, named(crowded, number // 4), named(ordinary, number - number // 4 - 1))
    mixed = jax.random.permutation(jax.random.fold_in(own, 3), number_of)
    source_of, taker = mixed[0:number_of // 2 * 2:2], mixed[1:number_of // 2 * 2:2]
    slack = jnp.minimum(tallies[source_of] - 1, limit - tallies[taker]) // 2
    slack = jnp.where((source_of == sequence[0]) | (taker == sequence[0]) | (tallies[taker] == 0), 0, jnp.maximum(slack, 0))
    moved = jax.random.randint(jax.random.fold_in(own, 4), (number_of // 2,), 0, 1 << 20) % (slack + 1)
    tallies = tallies.at[source_of].add(-moved).at[taker].add(moved)
    labels = jnp.searchsorted(jnp.cumsum(tallies), jnp.arange(rows * top), side="right").astype(jnp.int32)
    grid = labels.reshape(top, rows).T
    grid = grid[jax.random.permutation(jax.random.fold_in(own, 1), rows)]
    offset_by = jax.random.randint(jax.random.fold_in(own, 2), (rows, 1), 0, top)
    return jnp.take_along_axis(grid, (jnp.arange(top)[None, :] + offset_by) % top, axis=1)


def load_shares(amount, total, bound, skew, full):
    portions = [(1 << 20) // math.isqrt(standing ** skew) + 1 for standing in range(1, amount + 1)]
    largest = bound if full else min(bound, max(-(-total // amount), total * portions[0] // sum(portions)))
    least = 1 if total - largest >= amount - 1 else 0
    counts, surplus = [largest] + [least] * (amount - 1), total - largest - least * (amount - 1)
    while surplus > 0:
        free = [i for i in range(1, amount) if counts[i] < largest] or [i for i in range(1, amount) if counts[i] < bound]
        whole, budget = sum([portions[i] for i in free]), surplus
        for i in free:
            extra = min(bound - counts[i], max(1, budget * portions[i] // whole), surplus)
            counts[i] = counts[i] + extra
            surplus = surplus - extra
    return np.array(counts)


def scatter_about(own_key, dims, deviation, reach, cuts=(), kind=jnp.bfloat16):
    gain = levels(own_key, dims, cuts, -0.22, 0.18) if cuts else 1.0
    values = jax.random.normal(own_key, dims, jnp.float32) * deviation * gain
    return jnp.minimum(jnp.maximum(values, -reach), reach).astype(kind)


def setup_inputs(seed: int = 0) -> dict:
    seeds = jax.random.split(jax.random.key(seed), 8)
    tokens = scatter_about(seeds[0], (TOKENS, D), 1.0, 6.0, ((0, 128),))
    routes_keys = jax.random.split(jax.random.fold_in(seeds[1], 1), TOKENS // TOK_DEV)
    routes_turns = jax.random.permutation(jax.random.fold_in(seeds[1], 3), TOKENS // TOK_DEV)
    routes = jax.vmap(lambda own, number: assign_block(jax.random.fold_in(seeds[1], 2), own, number, TOK_DEV, ALL_EXP, TOPK, CAP, 2))(routes_keys, routes_turns).reshape((TOKENS, TOPK))
    route_weight = jnp.clip(jnp.exp(math.log(2.0) - 2.3025851 * jax.random.uniform(seeds[2], (TOKENS, TOPK), jnp.float32) ** levels(seeds[2], (TOKENS, TOPK), ((0, 128),), -0.2, 0.2)), 0.2, 2.0)
    w_gate = scatter_about(seeds[3], (EXPERTS, D, FFE), D ** -0.5, 0.0625, ((0, 16), (1, 8)))
    w_up = scatter_about(seeds[4], (EXPERTS, D, FFE), D ** -0.5, 0.0625, ((0, 16), (1, 8)))
    w_down = scatter_about(seeds[5], (EXPERTS, FFE, D), FFE ** -0.5, 0.1875, ((0, 16), (2, 8)))
    grad_out = scatter_about(seeds[6], (TOKENS, D), 1.0, 6.0, ((0, 128),))
    return {"tokens": tokens, "routes": routes, "route_weight": route_weight, "w_gate": w_gate, "w_up": w_up, "w_down": w_down, "grad_out": grad_out}


def silu_parts(gate_pre):
    sigmoid_g = jax.nn.sigmoid(gate_pre)
    return gate_pre * sigmoid_g, sigmoid_g * (1.0 + gate_pre * (1.0 - sigmoid_g))


def reference(tokens, routes, route_weight, w_gate, w_up, w_down, grad_out):
    block_count = TOKENS // TOK_DEV
    flat_routes = routes.reshape(block_count, TOK_DEV * TOPK)
    onehot = (flat_routes[:, :, None] == jnp.arange(EXPERTS, dtype=jnp.int32)[None, None, :]).astype(jnp.int32)
    before = jnp.sum((jnp.cumsum(onehot, axis=1) - onehot) * onehot, axis=2).astype(jnp.int32)
    block_ids = jnp.arange(block_count, dtype=jnp.int32)[:, None]
    slot_rows = block_count * CAP
    slot_ids = flat_routes * slot_rows + block_ids * CAP + before
    slot_ids = jnp.where(flat_routes < EXPERTS, slot_ids, EXPERTS * slot_rows).astype(jnp.int32)
    pick_ids = jnp.arange(TOKENS * TOPK, dtype=jnp.int32)
    table = jnp.full((EXPERTS * slot_rows,), -1, jnp.int32).at[slot_ids.reshape(-1)].set(pick_ids, mode="drop")
    weights_flat = route_weight.reshape(-1)

    def per_expert(state, expert):
        out_sum, grad_sum, route_sum = state
        entry = lax.dynamic_slice_in_dim(table, expert * slot_rows, slot_rows)
        filled = entry >= 0
        pick_safe = jnp.where(filled, entry, 0).astype(jnp.int32)
        token_ids = (pick_safe // TOPK).astype(jnp.int32)
        scale = jnp.where(filled, weights_flat[pick_safe], jnp.zeros((), jnp.float32))
        x_rows = jnp.where(filled[:, None], tokens[token_ids], jnp.zeros((), jnp.bfloat16))
        dy_rows = jnp.where(filled[:, None], grad_out[token_ids], jnp.zeros((), jnp.bfloat16)).astype(jnp.float32)
        do_rows = (scale[:, None] * dy_rows).astype(jnp.bfloat16)
        gate_w = w_gate[expert]
        up_w = w_up[expert]
        down_w = w_down[expert]
        gate_pre = jnp.dot(x_rows, gate_w, preferred_element_type=jnp.float32)
        up_value = jnp.dot(x_rows, up_w, preferred_element_type=jnp.float32)
        back_grad = jnp.dot(do_rows, down_w.T, preferred_element_type=jnp.float32)
        smooth, silu_slope = silu_parts(gate_pre)
        hidden = (smooth * up_value).astype(jnp.bfloat16)
        d_gate = (back_grad * up_value * silu_slope).astype(jnp.bfloat16)
        d_up = (back_grad * smooth).astype(jnp.bfloat16)
        expert_out = jnp.dot(hidden, down_w, preferred_element_type=jnp.float32).astype(jnp.bfloat16)
        grad_rows = (jnp.dot(d_gate, gate_w.T, preferred_element_type=jnp.float32)
                     + jnp.dot(d_up, up_w.T, preferred_element_type=jnp.float32)).astype(jnp.bfloat16)
        grad_gate = jnp.dot(x_rows.T, d_gate, preferred_element_type=jnp.float32).astype(jnp.bfloat16)
        grad_up = jnp.dot(x_rows.T, d_up, preferred_element_type=jnp.float32).astype(jnp.bfloat16)
        grad_down = jnp.dot(hidden.T, do_rows, preferred_element_type=jnp.float32).astype(jnp.bfloat16)
        targets = jnp.where(filled, token_ids, TOKENS).astype(jnp.int32)
        out_float = expert_out.astype(jnp.float32)
        out_sum = out_sum.at[targets].add(scale[:, None] * out_float, mode="drop")
        grad_sum = grad_sum.at[targets].add(grad_rows.astype(jnp.float32), mode="drop")
        pick_target = jnp.where(filled, entry, TOKENS * TOPK).astype(jnp.int32)
        route_sum = route_sum.at[pick_target].add(jnp.sum(dy_rows * out_float, axis=1), mode="drop")
        return (out_sum, grad_sum, route_sum), (grad_gate, grad_up, grad_down)

    initial = (jnp.zeros((TOKENS, D), jnp.float32), jnp.zeros((TOKENS, D), jnp.float32),
               jnp.zeros((TOKENS * TOPK,), jnp.float32))
    totals, weight_grads = lax.scan(per_expert, initial, jnp.arange(EXPERTS, dtype=jnp.int32))
    out_sum, grad_sum, route_sum = totals
    grad_gate, grad_up, grad_down = weight_grads
    return (out_sum.astype(jnp.bfloat16), grad_sum.astype(jnp.bfloat16), route_sum.reshape(TOKENS, TOPK),
            grad_gate, grad_up, grad_down)
```

```python
import functools

import jax
import jax.numpy as jnp
from jax import lax
from jax.experimental import pallas as pl
from jax.experimental.pallas import tpu as pltpu
from jax.sharding import Mesh, PartitionSpec as P

CAP = 6
PAD = 8
BF16 = jnp.bfloat16
F32 = jnp.float32
VMEM_LIMIT = 56 * 1024 * 1024


def dot(a, b, ca=1, cb=0):
    return lax.dot_general(a, b, (((ca,), (cb,)), ((), ())), preferred_element_type=F32)


def whole():
    return pl.BlockSpec(memory_space=pltpu.VMEM)


def smem():
    return pl.BlockSpec(memory_space=pltpu.SMEM)


def tail_slot(row, q):
    return jnp.where(row == 6, q, jnp.where(row == 7, 3 + q, -1))


def main_slot(row):
    return jnp.where(row < CAP, row, -1)


def prep_kernel(core_ref, routes_ref, weight_ref, tok_ref, go_ref, out_ref, sel_ref, wsel_ref, selt_s, scale_s):
    rows = routes_ref.shape[0]
    lanes = sel_ref.shape[2]
    half = tok_ref.shape[1] // 2

    @pl.when(pl.program_id(0) == 0)
    def _():
        lane = lax.broadcasted_iota(jnp.int32, (rows, lanes), 1)
        expert, row = lane >> 3, lane & 7
        named = jnp.zeros((rows, lanes), F32)
        weight = jnp.zeros((rows, lanes), F32)
        for k in range(routes_ref.shape[1]):
            hit = routes_ref[:, k : k + 1] == expert
            named = named + jnp.where(hit, 1.0, 0.0)
            weight = weight + jnp.where(hit, weight_ref[:, k : k + 1], 0.0)
        earlier = lax.broadcasted_iota(jnp.int32, (rows, rows), 1) < lax.broadcasted_iota(jnp.int32, (rows, rows), 0)
        before = dot(jnp.where(earlier, 1.0, 0.0).astype(BF16), named.astype(BF16))
        picked = []
        for want in [main_slot(row)] + [tail_slot(row, q) for q in range(3)]:
            picked.append(jnp.where((named > 0.5) & (before == want.astype(F32)), 1.0, 0.0))
        slot_row = lax.broadcasted_iota(jnp.int32, (lanes, 1), 0) & 7
        scales = []
        for i, one in enumerate(picked):
            sel_ref[i] = one.astype(BF16)
            selt_s[i] = one.T.astype(BF16)
            scales.append(jnp.sum((one * weight).T, axis=1, keepdims=True))
        plain = jnp.where(slot_row < CAP, 1.0, 0.0)
        scale_s[0] = plain + scales[1]
        scale_s[1] = plain + scales[2]
        scale_s[2] = scales[0] + scales[3]
        wsel = picked[0] * weight
        high = wsel.astype(BF16)
        wsel_ref[0] = high
        wsel_ref[1] = (wsel - high.astype(F32)).astype(BF16)

    own = pl.multiple_of(core_ref[0] * half, 128)
    other = pl.multiple_of((1 - core_ref[0]) * half, 128)
    tail = go_ref[:, pl.ds(other, half)]
    sources = (tok_ref[:, pl.ds(own, half)], tok_ref[:, pl.ds(other, half)], go_ref[:, pl.ds(own, half)])
    for q, source in enumerate(sources):
        rows_q = dot(selt_s[0], source) + dot(selt_s[1 + q], tail)
        out_ref[0, :, q * half : (q + 1) * half] = (scale_s[q] * rows_q).astype(BF16)


def prep(core, routes, route_weight, tokens, grad_out, quarters, experts):
    rows, width = tokens.shape
    lanes = experts * PAD
    quarter = width // quarters
    half = quarter // 2
    column = pl.BlockSpec((rows, quarter), lambda i: (0, i))
    return pl.pallas_call(
        prep_kernel,
        grid=(quarters,),
        in_specs=[smem(), whole(), whole(), column, column],
        out_specs=[
            pl.BlockSpec((1, lanes, 3 * half), lambda i: (i, 0, 0)),
            pl.BlockSpec((4, rows, lanes), lambda i: (0, 0, 0)),
            pl.BlockSpec((2, rows, lanes), lambda i: (0, 0, 0)),
        ],
        out_shape=[
            jax.ShapeDtypeStruct((quarters, lanes, 3 * half), BF16),
            jax.ShapeDtypeStruct((4, rows, lanes), BF16),
            jax.ShapeDtypeStruct((2, rows, lanes), BF16),
        ],
        scratch_shapes=[pltpu.VMEM((4, lanes, rows), BF16), pltpu.VMEM((3, lanes, 1), F32)],
        compiler_params=pltpu.CompilerParams(vmem_limit_bytes=VMEM_LIMIT),
        cost_estimate=pl.CostEstimate(flops=800_000_000, bytes_accessed=6_500_000, transcendentals=0),
        name="prep",
    )(core, routes, route_weight, tokens, grad_out)


def slot_masks(slots, lanes, transposed=False):
    shape = (lanes, slots) if transposed else (slots, lanes)
    slot_dim, lane_dim = (1, 0) if transposed else (0, 1)
    slot = lax.broadcasted_iota(jnp.int32, shape, slot_dim)
    lane = lax.broadcasted_iota(jnp.int32, shape, lane_dim)
    expert = (slot * 43) >> 8
    place = slot - expert * CAP
    row = lane & 7
    same = (lane >> 3) == expert
    wants = [main_slot(row)] + [tail_slot(row, q) for q in range(3)]
    return [jnp.where(same & (place == want), 1.0, 0.0).astype(BF16) for want in wants]


def first_kernel(at_ref, recv_ref, go_ref, gx_ref, uo_ref, ux_ref, do_ref, dx_ref, p0_ref, p1_ref, p2_ref, p3_ref, own_ref, other_ref):
    quarters, lanes, packed = recv_ref.shape
    half = packed // 3
    slots = p0_ref.shape[1]

    @pl.when(pl.program_id(0) == 0)
    def _():
        masks = slot_masks(slots, lanes)
        for j in range(quarters):
            source = lax.rem(at_ref[0] + j, quarters)
            rows = pl.ds(j * slots, slots)
            block = [recv_ref[source, :, q * half : (q + 1) * half] for q in range(3)]
            own_ref[0, rows, :] = dot(masks[0], block[0]).astype(BF16)
            other_ref[0, rows, :] = dot(masks[0], block[1]).astype(BF16)
            own_ref[1, rows, :] = dot(masks[0], block[2]).astype(BF16)
            tail = dot(masks[1], block[0]) + dot(masks[2], block[1]) + dot(masks[3], block[2])
            other_ref[1, rows, :] = tail.astype(BF16)

    gate = dot(own_ref[0], go_ref[...]) + dot(other_ref[0], gx_ref[...])
    up = dot(own_ref[0], uo_ref[...]) + dot(other_ref[0], ux_ref[...])
    back = dot(own_ref[1], do_ref[...], 1, 1) + dot(other_ref[1], dx_ref[...], 1, 1)
    for i, value in enumerate((gate, up, back)):
        p0_ref[i] = value[0:slots]
        p1_ref[i] = value[slots : 2 * slots].astype(BF16)
        p2_ref[i] = value[2 * slots : 3 * slots].astype(BF16)
        p3_ref[i] = value[3 * slots :].astype(BF16)


def first(at, recv, weights, hidden, slots):
    quarters, lanes, packed = recv.shape
    half = packed // 3
    step = 256
    up_spec = pl.BlockSpec((half, step), lambda n: (0, n))
    down_spec = pl.BlockSpec((step, half), lambda n: (n, 0))
    part = pl.BlockSpec((3, slots, step), lambda n: (0, 0, n))
    kept = pl.BlockSpec((2, quarters * slots, half), lambda n: (0, 0, 0))
    return pl.pallas_call(
        first_kernel,
        grid=(hidden // step,),
        in_specs=[smem(), whole()] + [up_spec] * 4 + [down_spec] * 2,
        out_specs=[part] * 4 + [kept] * 2,
        out_shape=[jax.ShapeDtypeStruct((3, slots, hidden), F32)]
        + [jax.ShapeDtypeStruct((3, slots, hidden), BF16)] * 3
        + [jax.ShapeDtypeStruct((2, quarters * slots, half), BF16)] * 2,
        compiler_params=pltpu.CompilerParams(vmem_limit_bytes=VMEM_LIMIT),
        cost_estimate=pl.CostEstimate(flops=6_000_000_000, bytes_accessed=20_000_000, transcendentals=0),
        name="first",
    )(at, recv, *weights)


def activate(p0, others):
    total = p0
    for one in others:
        total = total + one.astype(F32)
    gate, up, back = total[0], total[1], total[2]
    sig = jax.nn.sigmoid(gate)
    smooth = gate * sig
    slope = sig * (1.0 + gate * (1.0 - sig))
    return jnp.stack([(smooth * up).astype(BF16), (back * up * slope).astype(BF16), (back * smooth).astype(BF16)])


def second_kernel(at_ref, h0_ref, h1_ref, h2_ref, h3_ref, do_ref, dx_ref, go_ref, gx_ref, uo_ref, ux_ref, out_ref, all_s):
    quarters, lanes, packed = out_ref.shape
    half = packed // 3
    slots = h0_ref.shape[1]
    for j, h_ref in enumerate((h0_ref, h1_ref, h2_ref, h3_ref)):
        for i in range(3):
            all_s[i, j * slots : (j + 1) * slots, :] = h_ref[i]
    masks = slot_masks(slots, lanes, True)
    a_own = dot(all_s[0], do_ref[...]).astype(BF16)
    a_other = dot(all_s[0], dx_ref[...]).astype(BF16)
    b_own = (dot(all_s[1], go_ref[...], 1, 1) + dot(all_s[2], uo_ref[...], 1, 1)).astype(BF16)
    b_other = (dot(all_s[1], gx_ref[...], 1, 1) + dot(all_s[2], ux_ref[...], 1, 1)).astype(BF16)
    for j in range(quarters):
        target = lax.rem(at_ref[0] + j, quarters)
        rows = slice(j * slots, (j + 1) * slots)
        for q, value in enumerate((a_own, a_other, b_own)):
            packed_rows = dot(masks[0], value[rows]) + dot(masks[1 + q], b_other[rows])
            out_ref[target, :, q * half : (q + 1) * half] = packed_rows.astype(BF16)


def second(at, parts, weights, lanes):
    quarters = len(parts)
    _, slots, hidden = parts[0].shape
    half = weights[0].shape[1]
    return pl.pallas_call(
        second_kernel,
        in_specs=[smem()] + [whole()] * 10,
        out_specs=whole(),
        out_shape=jax.ShapeDtypeStruct((quarters, lanes, 3 * half), BF16),
        scratch_shapes=[pltpu.VMEM((3, quarters * slots, hidden), BF16)],
        compiler_params=pltpu.CompilerParams(vmem_limit_bytes=VMEM_LIMIT),
        cost_estimate=pl.CostEstimate(flops=5_000_000_000, bytes_accessed=16_000_000, transcendentals=0),
        name="second",
    )(at, *parts, *weights)


def last_kernel(core_ref, routes_ref, sel_ref, wsel_ref, recv_ref, go_ref, moe_ref, gt_ref, gr_ref, inner_s):
    step = pl.program_id(0)
    half = go_ref.shape[1] // 2
    own = pl.ds(pl.multiple_of(core_ref[0] * half, 128), half)
    other = pl.ds(pl.multiple_of((1 - core_ref[0]) * half, 128), half)
    block = [recv_ref[0, :, q * half : (q + 1) * half] for q in range(3)]
    moe_ref[:, own] = (dot(wsel_ref[0], block[0]) + dot(wsel_ref[1], block[0])).astype(BF16)
    moe_ref[:, other] = (dot(wsel_ref[0], block[1]) + dot(wsel_ref[1], block[1])).astype(BF16)
    gt_ref[:, own] = dot(sel_ref[0], block[2]).astype(BF16)
    gt_ref[:, other] = (dot(sel_ref[1], block[0]) + dot(sel_ref[2], block[1]) + dot(sel_ref[3], block[2])).astype(BF16)
    inner = dot(go_ref[:, own], block[0], 1, 1) + dot(go_ref[:, other], block[1], 1, 1)

    @pl.when(step == 0)
    def _():
        inner_s[...] = inner

    @pl.when(step > 0)
    def _():
        inner_s[...] += inner

    @pl.when(step == pl.num_programs(0) - 1)
    def _():
        rows, picks = routes_ref.shape
        lanes = sel_ref.shape[2]
        expert = lax.broadcasted_iota(jnp.int32, (rows, lanes), 1) >> 3
        column = lax.broadcasted_iota(jnp.int32, (rows, picks), 1)
        held = sel_ref[0].astype(F32) * inner_s[...]
        out = jnp.zeros((rows, picks), F32)
        for k in range(picks):
            mine = jnp.sum(jnp.where(routes_ref[:, k : k + 1] == expert, held, 0.0), axis=1, keepdims=True)
            out = out + jnp.where(column == k, mine, 0.0)
        gr_ref[...] = out


def last(core, routes, sel, wsel, recv, grad_out):
    rows, width = grad_out.shape
    quarters, lanes, packed = recv.shape
    column = pl.BlockSpec((rows, width // quarters), lambda i: (0, i))
    return pl.pallas_call(
        last_kernel,
        grid=(quarters,),
        in_specs=[smem(), whole(), whole(), whole(), pl.BlockSpec((1, lanes, packed), lambda i: (i, 0, 0)), column],
        out_specs=[column, column, pl.BlockSpec(routes.shape, lambda i: (0, 0))],
        out_shape=[
            jax.ShapeDtypeStruct((rows, width), BF16),
            jax.ShapeDtypeStruct((rows, width), BF16),
            jax.ShapeDtypeStruct(routes.shape, F32),
        ],
        scratch_shapes=[pltpu.VMEM((rows, lanes), F32)],
        compiler_params=pltpu.CompilerParams(vmem_limit_bytes=VMEM_LIMIT),
        cost_estimate=pl.CostEstimate(flops=1_500_000_000, bytes_accessed=8_500_000, transcendentals=0),
        name="last",
    )(core, routes, sel, wsel, recv, grad_out)


def on_device(tokens, routes, route_weight, w_gate, w_up, w_down, grad_out):
    quarters = lax.axis_size("y")
    experts = lax.axis_size("x") * lax.axis_size("z")
    slots = experts * CAP
    lanes = experts * PAD
    hidden = w_gate.shape[2]
    everyone = ("y", "x", "z")
    core = lax.axis_index("k").astype(jnp.int32).reshape(1)
    at = lax.axis_index("y").astype(jnp.int32).reshape(1)

    def to_partner(value):
        return lax.ppermute(value, "k", [(0, 1), (1, 0)])

    def along(value, shift):
        return lax.ppermute(value, "y", [(i, (i + shift) % quarters) for i in range(quarters)])

    def exchange(value):
        flat = value.reshape(quarters * experts, PAD, value.shape[2])
        return lax.all_to_all(flat, everyone, 0, 0, tiled=True).reshape(value.shape)

    gate_own, up_own, down_own = w_gate[0], w_up[0], w_down[0]
    gate_other, up_other, down_other = to_partner(gate_own), to_partner(up_own), to_partner(down_own)

    sent, sel, wsel = prep(core, routes, route_weight, tokens, grad_out, quarters, experts)
    recv = exchange(sent)
    p0, p1, p2, p3, rows_own, rows_other = first(
        at, recv, (gate_own, gate_other, up_own, up_other, down_own, down_other), hidden, slots
    )
    others = [along(p2, 2), along(p1, 1), along(p3, 3)]
    rows_partner = to_partner(rows_other)
    mine = activate(p0, others)
    parts = [mine, along(mine, 3), along(mine, 2), along(mine, 1)]
    back = exchange(second(at, parts, (down_own, down_other, gate_own, gate_other, up_own, up_other), lanes))

    parts_partner = [to_partner(one) for one in parts]
    x_all = jnp.concatenate([rows_own[0], rows_partner[0]], axis=0)
    d_all = jnp.concatenate([rows_own[1], rows_partner[1]], axis=0)
    h_all, dg_all, du_all = (jnp.concatenate([one[i] for one in parts + parts_partner], axis=0) for i in range(3))
    grad_gate = dot(x_all, dg_all, 0, 0).astype(BF16)
    grad_up = dot(x_all, du_all, 0, 0).astype(BF16)
    grad_down = dot(h_all, d_all, 0, 0).astype(BF16)

    moe_out, grad_tokens, grad_route = last(core, routes, sel, wsel, back, grad_out)
    return (moe_out, grad_tokens, grad_route, grad_gate[None], grad_up[None], grad_down[None])


def solution(mesh):
    ctx, head = mesh.shape["ctx"], mesh.shape["head"]
    side = int(round(ctx**0.5))
    fine = Mesh(mesh.devices.reshape(side, ctx // side, head // 2, 2), ("x", "z", "y", "k"))
    e, d, both = ("x", "z"), ("y", "k"), ("x", "z", "y", "k")
    rows = P(both, None)
    up, down = P(e, d, None), P(e, None, d)
    return jax.shard_map(
        on_device,
        mesh=fine,
        in_specs=(rows, rows, rows, up, up, down, rows),
        out_specs=(rows, rows, rows, up, up, down),
        check_vma=False,
    )
```

```python
import functools

import jax
import jax.numpy as jnp
from jax import lax
from jax.experimental import pallas as pl
from jax.experimental.pallas import tpu as pltpu
from jax.sharding import Mesh, PartitionSpec as P

CAP = 6
PAD = 8
BF16 = jnp.bfloat16
F32 = jnp.float32
VMEM_LIMIT = 32 * 1024 * 1024
SMALL_LIMIT = 32 * 1024 * 1024
BIG_LIMIT = 60 * 1024 * 1024


def dot(a, b, ca=1, cb=0):
    return lax.dot_general(a, b, (((ca,), (cb,)), ((), ())), preferred_element_type=F32)


def whole():
    return pl.BlockSpec(memory_space=pltpu.VMEM)


def hbm():
    return pl.BlockSpec(memory_space=pltpu.HBM)


def start(pairs, sems):
    copies = [pltpu.make_async_copy(src, dst, sems.at[i]) for i, (src, dst) in enumerate(pairs)]
    for one in copies:
        one.start()
    return copies


def smem():
    return pl.BlockSpec(memory_space=pltpu.SMEM)


def tail_slot(row, q):
    return jnp.where(row == 6, q, jnp.where(row == 7, 3 + q, -1))


def main_slot(row):
    return jnp.where(row < CAP, row, -1)


def prep_kernel(core_ref, routes_ref, weight_ref, tok_ref, go_ref, out_ref, sel_ref, wsel_ref, scale_s):
    picks, rows = routes_ref.shape
    lanes = sel_ref.shape[1]
    half = tok_ref.shape[1] // 2

    @pl.when(pl.program_id(0) == 0)
    def _():
        slot = lax.broadcasted_iota(jnp.int32, (lanes, rows), 0)
        expert, row = slot >> 3, slot & 7
        named = jnp.zeros((lanes, rows), F32)
        weight = jnp.zeros((lanes, rows), F32)
        for k in range(picks):
            hit = routes_ref[k : k + 1, :] == expert
            named = named + jnp.where(hit, 1.0, 0.0)
            weight = weight + jnp.where(hit, weight_ref[k : k + 1, :], 0.0)
        earlier = lax.broadcasted_iota(jnp.int32, (rows, rows), 0) < lax.broadcasted_iota(jnp.int32, (rows, rows), 1)
        before = dot(named.astype(BF16), jnp.where(earlier, 1.0, 0.0).astype(BF16))
        picked, scales = [], []
        for i, want in enumerate([main_slot(row)] + [tail_slot(row, q) for q in range(3)]):
            one = jnp.where((named > 0.5) & (before == want.astype(F32)), 1.0, 0.0)
            sel_ref[i] = one.astype(BF16)
            picked.append(one)
            scales.append(jnp.sum(one * weight, axis=1, keepdims=True))
        plain = jnp.where((lax.broadcasted_iota(jnp.int32, (lanes, 1), 0) & 7) < CAP, 1.0, 0.0)
        scale_s[0] = plain + scales[1]
        scale_s[1] = plain + scales[2]
        scale_s[2] = scales[0] + scales[3]
        wsel = picked[0] * weight
        high = wsel.astype(BF16)
        wsel_ref[0] = high
        wsel_ref[1] = (wsel - high.astype(F32)).astype(BF16)

    own = pl.multiple_of(core_ref[0] * half, 128)
    other = pl.multiple_of((1 - core_ref[0]) * half, 128)
    tail = go_ref[:, pl.ds(other, half)]
    sources = (tok_ref[:, pl.ds(own, half)], tok_ref[:, pl.ds(other, half)], go_ref[:, pl.ds(own, half)])
    for q, source in enumerate(sources):
        rows_q = dot(sel_ref[0], source) + dot(sel_ref[1 + q], tail)
        out_ref[0, :, q * half : (q + 1) * half] = (scale_s[q] * rows_q).astype(BF16)


def prep(core, routes, route_weight, tokens, grad_out, quarters, experts):
    rows, width = tokens.shape
    lanes = experts * PAD
    quarter = width // quarters
    half = quarter // 2
    column = pl.BlockSpec((rows, quarter), lambda i: (0, i))
    return pl.pallas_call(
        prep_kernel,
        grid=(quarters,),
        in_specs=[smem(), whole(), whole(), column, column],
        out_specs=[
            pl.BlockSpec((1, lanes, 3 * half), lambda i: (i, 0, 0)),
            pl.BlockSpec((4, lanes, rows), lambda i: (0, 0, 0)),
            pl.BlockSpec((2, lanes, rows), lambda i: (0, 0, 0)),
        ],
        out_shape=[
            jax.ShapeDtypeStruct((quarters, lanes, 3 * half), BF16),
            jax.ShapeDtypeStruct((4, lanes, rows), BF16),
            jax.ShapeDtypeStruct((2, lanes, rows), BF16),
        ],
        scratch_shapes=[pltpu.VMEM((3, lanes, 1), F32)],
        compiler_params=pltpu.CompilerParams(vmem_limit_bytes=BIG_LIMIT),
        cost_estimate=pl.CostEstimate(flops=800_000_000, bytes_accessed=6_500_000, transcendentals=0),
        name="prep",
    )(core, routes, route_weight, tokens, grad_out)


def slot_masks(slots, lanes, transposed=False):
    shape = (lanes, slots) if transposed else (slots, lanes)
    slot_dim, lane_dim = (1, 0) if transposed else (0, 1)
    slot = lax.broadcasted_iota(jnp.int32, shape, slot_dim)
    lane = lax.broadcasted_iota(jnp.int32, shape, lane_dim)
    expert = (slot * 171) >> 10
    place = slot - expert * CAP
    row = lane & 7
    same = (lane >> 3) == expert
    wants = [main_slot(row)] + [tail_slot(row, q) for q in range(3)]
    return [jnp.where(same & (place == want), 1.0, 0.0).astype(BF16) for want in wants]


def pair_of(ref, p, columns):
    return jnp.concatenate([ref[2 * p, :, columns], ref[2 * p + 1, :, columns]], axis=0)


def share_out(at_ref, total_s, outs):
    quarters = len(outs)
    slots = outs[0].shape[0]
    for j, out in enumerate(outs):
        rows = pl.ds(pl.multiple_of(lax.rem(at_ref[0] + j, quarters) * slots, 32), slots)
        out[...] = total_s[rows, :].astype(out.dtype)


def gate_kernel(at_ref, recv_any, wo_ref, wx_ref, p0_ref, p1_ref, p2_ref, p3_ref, own_ref, other_ref, kept_any, total_s, recv_s, sems):
    quarters, lanes, _ = recv_any.shape
    half = wo_ref.shape[0]
    slots = p0_ref.shape[0]
    pairs = quarters // 2
    copies = start([(recv_any.at[pl.ds(2 * p, 2), :, pl.ds(0, 2 * half)], recv_s.at[p]) for p in range(pairs)], sems)
    main = slot_masks(2 * slots, 2 * lanes)[0]
    for p in range(pairs):
        rows = slice(2 * p * slots, 2 * (p + 1) * slots)
        copies[p].wait()
        block = jnp.concatenate([recv_s[p, 0], recv_s[p, 1]], axis=0)
        own_ref[rows, :] = dot(main, block[:, :half]).astype(BF16)
        other_ref[rows, :] = dot(main, block[:, half:]).astype(BF16)
    total_s[...] = dot(own_ref[...], wo_ref[...]) + dot(other_ref[...], wx_ref[...])
    share_out(at_ref, total_s, (p0_ref, p1_ref, p2_ref, p3_ref))


def up_kernel(at_ref, own_ref, other_ref, wo_ref, wx_ref, p0_ref, p1_ref, p2_ref, p3_ref, total_s):
    total_s[...] = dot(own_ref[...], wo_ref[...]) + dot(other_ref[...], wx_ref[...])
    share_out(at_ref, total_s, (p0_ref, p1_ref, p2_ref, p3_ref))


def back_kernel(at_ref, recv_ref, wo_ref, wx_ref, p0_ref, p1_ref, p2_ref, p3_ref, own_ref, other_ref, total_s):
    quarters, lanes, _ = recv_ref.shape
    half = wo_ref.shape[1]
    slots = p0_ref.shape[0]
    masks = slot_masks(2 * slots, 2 * lanes)
    for p in range(quarters // 2):
        rows = slice(2 * p * slots, 2 * (p + 1) * slots)
        blocks = [pair_of(recv_ref, p, slice(q * half, (q + 1) * half)) for q in range(3)]
        own_ref[rows, :] = dot(masks[0], blocks[2]).astype(BF16)
        other_ref[rows, :] = sum(dot(masks[1 + q], blocks[q]) for q in range(3)).astype(BF16)
    total_s[...] = dot(own_ref[...], wo_ref[...], 1, 1) + dot(other_ref[...], wx_ref[...], 1, 1)
    share_out(at_ref, total_s, (p0_ref, p1_ref, p2_ref, p3_ref))


def projection(kernel, name, at, rows, weights, over, slots, quarters):
    half, hidden = weights[0].shape[over], weights[0].shape[1 - over]
    outs = [jax.ShapeDtypeStruct((slots, hidden), F32 if j == 0 else BF16) for j in range(quarters)]
    scratch = [pltpu.VMEM((quarters * slots, hidden), F32)]
    if len(rows) == 1:
        outs = outs + [jax.ShapeDtypeStruct((quarters * slots, half), BF16)] * 2
    in_specs = [smem()] + [whole()] * (len(rows) + 2)
    out_specs = [whole()] * len(outs)
    aliases = {}
    if kernel is gate_kernel:
        anywhere = pl.BlockSpec(memory_space=pl.ANY)
        in_specs[1] = anywhere
        outs.append(jax.ShapeDtypeStruct(rows[0].shape, BF16))
        out_specs.append(anywhere)
        aliases = {1: len(outs) - 1}
        scratch += [
            pltpu.VMEM((quarters // 2, 2, rows[0].shape[1], 2 * half), BF16),
            pltpu.SemaphoreType.DMA((quarters // 2,)),
        ]
    return pl.pallas_call(
        kernel,
        in_specs=in_specs,
        out_specs=out_specs,
        out_shape=outs,
        scratch_shapes=scratch,
        input_output_aliases=aliases,
        compiler_params=pltpu.CompilerParams(vmem_limit_bytes=VMEM_LIMIT),
        cost_estimate=pl.CostEstimate(flops=3_000_000_000, bytes_accessed=8_000_000, transcendentals=0),
        name=name,
    )(at, *rows, *weights)


def gather_parts(at_ref, parts, all_s):
    quarters = len(parts)
    slots = parts[0].shape[0]
    for j, part in enumerate(parts):
        rows = pl.ds(pl.multiple_of(lax.rem(at_ref[0] + j, quarters) * slots, 32), slots)
        all_s[rows, :] = part[...]


def out_kernel(at_ref, h0, h1, h2, h3, wo_ref, wx_ref, out_ref, all_ref):
    quarters, lanes, width = out_ref.shape
    half = width // 2
    slots = h0.shape[0]
    gather_parts(at_ref, (h0, h1, h2, h3), all_ref)
    main = slot_masks(2 * slots, 2 * lanes, True)[0]
    for q, w_ref in enumerate((wo_ref, wx_ref)):
        value = dot(all_ref[...], w_ref[...]).astype(BF16)
        for p in range(quarters // 2):
            rows = dot(main, value[2 * p * slots : 2 * (p + 1) * slots]).astype(BF16)
            out_ref[2 * p, :, q * half : (q + 1) * half] = rows[:lanes]
            out_ref[2 * p + 1, :, q * half : (q + 1) * half] = rows[lanes:]


def out_rows(at, parts, weights, lanes):
    quarters = len(parts)
    slots, hidden = parts[0].shape
    half = weights[0].shape[1]
    return pl.pallas_call(
        out_kernel,
        in_specs=[smem()] + [whole()] * (quarters + 2),
        out_specs=[whole()] * 2,
        out_shape=[
            jax.ShapeDtypeStruct((quarters, lanes, 2 * half), BF16),
            jax.ShapeDtypeStruct((quarters * slots, hidden), BF16),
        ],
        compiler_params=pltpu.CompilerParams(vmem_limit_bytes=VMEM_LIMIT),
        cost_estimate=pl.CostEstimate(flops=2_000_000_000, bytes_accessed=7_500_000, transcendentals=0),
        name="out_rows",
    )(at, *parts, *weights)


def grad_kernel(at_ref, g0, g1, g2, g3, main_ref, go_ref, gx_ref, uo_ref, ux_ref, out_ref, keep_hbm, all_s, sem):
    quarters, lanes, packed = out_ref.shape
    half = packed // 3
    slots = g0.shape[0]
    hidden = all_s.shape[1] // 2
    gather_parts(at_ref, (g0, g1, g2, g3), all_s)
    keep = pltpu.make_async_copy(all_s, keep_hbm, sem)
    keep.start()
    masks = slot_masks(2 * slots, 2 * lanes, True)
    dg, du = all_s[:, :hidden], all_s[:, hidden:]
    own = (dot(dg, go_ref[...], 1, 1) + dot(du, uo_ref[...], 1, 1)).astype(BF16)
    other = (dot(dg, gx_ref[...], 1, 1) + dot(du, ux_ref[...], 1, 1)).astype(BF16)
    for p in range(quarters // 2):
        rows = slice(2 * p * slots, 2 * (p + 1) * slots)
        for q in range(3):
            columns = slice(q * half, (q + 1) * half)
            value = dot(masks[1 + q], other[rows])
            if q == 2:
                value = value + dot(masks[0], own[rows])
            else:
                mine = jnp.concatenate([main_ref[2 * p, :, columns], main_ref[2 * p + 1, :, columns]], axis=0)
                value = value + mine.astype(F32)
            value = value.astype(BF16)
            out_ref[2 * p, :, columns] = value[:lanes]
            out_ref[2 * p + 1, :, columns] = value[lanes:]
    keep.wait()


def grad_rows(at, parts, main, weights):
    quarters, lanes, width = main.shape
    slots, both = parts[0].shape
    packed = width // 2 * 3
    return pl.pallas_call(
        grad_kernel,
        in_specs=[smem()] + [whole()] * (quarters + 5),
        out_specs=[whole(), hbm()],
        out_shape=[
            jax.ShapeDtypeStruct((quarters, lanes, packed), BF16),
            jax.ShapeDtypeStruct((quarters * slots, both), BF16),
        ],
        scratch_shapes=[
            pltpu.VMEM((quarters * slots, both), BF16),
            pltpu.SemaphoreType.DMA,
        ],
        compiler_params=pltpu.CompilerParams(vmem_limit_bytes=SMALL_LIMIT),
        cost_estimate=pl.CostEstimate(flops=3_500_000_000, bytes_accessed=14_000_000, transcendentals=0),
        name="grad_rows",
    )(at, *parts, main, *weights)


def weight_kernel(am_ref, ap_ref, bm_ref, bp_ref, out_ref):
    out_ref[...] = (dot(am_ref[...], bm_ref[...], 0, 0) + dot(ap_ref[...], bp_ref[...], 0, 0)).astype(BF16)


def weight_grad(a_mine, a_partner, b_mine, b_partner, step, at=0, columns=None):
    slots, rows = a_mine.shape
    columns = columns or b_mine.shape[1]
    a_spec = pl.BlockSpec((slots, rows), lambda n: (0, 0))
    b_spec = pl.BlockSpec((slots, step), lambda n: (0, n + at))
    return pl.pallas_call(
        weight_kernel,
        grid=(columns // step,),
        in_specs=[a_spec, a_spec, b_spec, b_spec],
        out_specs=pl.BlockSpec((rows, step), lambda n: (0, n)),
        out_shape=jax.ShapeDtypeStruct((rows, columns), BF16),
        compiler_params=pltpu.CompilerParams(vmem_limit_bytes=VMEM_LIMIT),
        cost_estimate=pl.CostEstimate(flops=1_500_000_000, bytes_accessed=5_000_000, transcendentals=0),
        name="weight_grad",
    )(a_mine, a_partner, b_mine, b_partner)


def last_kernel(core_ref, routes_ref, sel_ref, wsel_ref, recv_ref, go_ref, moe_ref, gt_ref, gr_ref, inner_s):
    step = pl.program_id(0)
    half = go_ref.shape[1] // 2
    own = pl.ds(pl.multiple_of(core_ref[0] * half, 128), half)
    other = pl.ds(pl.multiple_of((1 - core_ref[0]) * half, 128), half)
    block = [recv_ref[0, :, q * half : (q + 1) * half] for q in range(3)]
    moe_ref[:, own] = (dot(wsel_ref[0], block[0], 0, 0) + dot(wsel_ref[1], block[0], 0, 0)).astype(BF16)
    moe_ref[:, other] = (dot(wsel_ref[0], block[1], 0, 0) + dot(wsel_ref[1], block[1], 0, 0)).astype(BF16)
    gt_ref[:, own] = dot(sel_ref[0], block[2], 0, 0).astype(BF16)
    gt_ref[:, other] = sum(dot(sel_ref[1 + q], block[q], 0, 0) for q in range(3)).astype(BF16)
    inner = dot(block[0], go_ref[:, own], 1, 1) + dot(block[1], go_ref[:, other], 1, 1)

    @pl.when(step == 0)
    def _():
        inner_s[...] = inner

    @pl.when(step > 0)
    def _():
        inner_s[...] += inner

    @pl.when(step == pl.num_programs(0) - 1)
    def _():
        picks, rows = routes_ref.shape
        lanes = sel_ref.shape[1]
        expert = lax.broadcasted_iota(jnp.int32, (lanes, rows), 0) >> 3
        held = sel_ref[0].astype(F32) * inner_s[...]
        for k in range(picks):
            mine = jnp.where(routes_ref[k : k + 1, :] == expert, held, 0.0)
            gr_ref[k : k + 1, :] = jnp.sum(mine, axis=0, keepdims=True)


def last(core, routes, sel, wsel, recv, grad_out):
    rows, width = grad_out.shape
    quarters, lanes, packed = recv.shape
    column = pl.BlockSpec((rows, width // quarters), lambda i: (0, i))
    return pl.pallas_call(
        last_kernel,
        grid=(quarters,),
        in_specs=[smem(), whole(), whole(), whole(), pl.BlockSpec((1, lanes, packed), lambda i: (i, 0, 0)), column],
        out_specs=[column, column, pl.BlockSpec(routes.shape, lambda i: (0, 0))],
        out_shape=[
            jax.ShapeDtypeStruct((rows, width), BF16),
            jax.ShapeDtypeStruct((rows, width), BF16),
            jax.ShapeDtypeStruct(routes.shape, F32),
        ],
        scratch_shapes=[pltpu.VMEM((lanes, rows), F32)],
        compiler_params=pltpu.CompilerParams(vmem_limit_bytes=BIG_LIMIT),
        cost_estimate=pl.CostEstimate(flops=1_500_000_000, bytes_accessed=8_500_000, transcendentals=0),
        name="last",
    )(core, routes, sel, wsel, recv, grad_out)


def on_device(tokens, routes, route_weight, w_gate, w_up, w_down, grad_out):
    quarters = lax.axis_size("y")
    experts = lax.axis_size("x") * lax.axis_size("z")
    slots = experts * CAP
    lanes = experts * PAD
    hidden = w_gate.shape[2]
    everyone = ("y", "x", "z")
    half = w_gate.shape[1]
    core = lax.axis_index("k").astype(jnp.int32).reshape(1)
    at = lax.axis_index("y").astype(jnp.int32).reshape(1)

    def to_partner(value):
        return lax.ppermute(value, "k", [(0, 1), (1, 0)])

    def along(value, shift):
        return lax.ppermute(value, "y", [(i, (i + shift) % quarters) for i in range(quarters)])

    def exchange(value):
        flat = value.reshape(quarters * experts, PAD, value.shape[2])
        return lax.all_to_all(flat, everyone, 0, 0, tiled=True).reshape(value.shape)

    def add_over_y(shares):
        total = shares[0]
        for j in (2, 1, 3):
            total = total + along(shares[j], j).astype(F32)
        return total

    def from_y(value):
        return [value] + [along(value, quarters - j) for j in range(1, quarters)]

    gate_own, up_own, down_own = w_gate[0], w_up[0], w_down[0]
    gate_other, up_other, down_other = to_partner(gate_own), to_partner(up_own), to_partner(down_own)
    routes, route_weight = routes.T, route_weight.T

    sent, sel, wsel = prep(core, routes, route_weight, tokens, grad_out, quarters, experts)
    recv = exchange(sent)
    down = (down_own, down_other)
    *shares, x_own, x_other, recv = projection(gate_kernel, "gate", at, (recv,), (gate_own, gate_other), 0, slots, quarters)
    gate = add_over_y(shares)
    shares = projection(up_kernel, "up", at, (x_own, x_other), (up_own, up_other), 0, slots, quarters)
    up = add_over_y(shares)
    *shares, d_own, d_other = projection(back_kernel, "back", at, (recv,), down, 1, slots, quarters)
    back = add_over_y(shares)

    sig = jax.nn.sigmoid(gate)
    smooth = gate * sig
    slope = up * (sig * (1.0 + gate * (1.0 - sig)))
    mine, smooth, slope = lax.optimization_barrier(((smooth * up).astype(BF16), smooth, slope))
    h_parts = from_y(mine)
    back, h_parts = lax.optimization_barrier((back, h_parts))
    g_parts = from_y(jnp.concatenate([(back * slope).astype(BF16), (back * smooth).astype(BF16)], axis=1))
    main, h_mine = out_rows(at, h_parts, down, lanes)
    packed, g_mine = grad_rows(at, g_parts, main, (gate_own, gate_other, up_own, up_other))
    x_other, d_other, h_mine, g_mine = lax.optimization_barrier((x_other, d_other, h_mine, g_mine))
    returned = exchange(packed)

    x_partner, d_partner, h_partner = to_partner(x_other), to_partner(d_other), to_partner(h_mine)
    g_partner = to_partner(g_mine)
    step = hidden // 4
    grad_down = weight_grad(h_mine, h_partner, d_own, d_partner, half)
    grad_gate = weight_grad(x_own, x_partner, g_mine, g_partner, step, 0, hidden)
    grad_up = weight_grad(x_own, x_partner, g_mine, g_partner, step, 4, hidden)
    returned, grad_gate, grad_up, grad_down = lax.optimization_barrier((returned, grad_gate, grad_up, grad_down))

    moe_out, grad_tokens, grad_route = last(core, routes, sel, wsel, returned, grad_out)
    return (moe_out, grad_tokens, grad_route.T, grad_gate[None], grad_up[None], grad_down[None])


def solution(mesh):
    ctx, head = mesh.shape["ctx"], mesh.shape["head"]
    side = int(round(ctx**0.5))
    fine = Mesh(mesh.devices.reshape(side, ctx // side, head // 2, 2), ("x", "z", "y", "k"))
    e, d, both = ("x", "z"), ("y", "k"), ("x", "z", "y", "k")
    rows = P(both, None)
    up, down = P(e, d, None), P(e, None, d)
    return jax.shard_map(
        on_device,
        mesh=fine,
        in_specs=(rows, rows, rows, up, up, down, rows),
        out_specs=(rows, rows, rows, up, up, down),
        check_vma=False,
    )
```

```python
import functools

import jax
import jax.numpy as jnp
from jax import lax
from jax.experimental import pallas as pl
from jax.experimental.pallas import tpu as pltpu
from jax.sharding import Mesh, PartitionSpec as P

CAP = 6
PAD = 8
BF16 = jnp.bfloat16
F32 = jnp.float32
VMEM_LIMIT = 32 * 1024 * 1024
SMALL_LIMIT = 32 * 1024 * 1024
BIG_LIMIT = 60 * 1024 * 1024


def dot(a, b, ca=1, cb=0):
    return lax.dot_general(a, b, (((ca,), (cb,)), ((), ())), preferred_element_type=F32)


def whole():
    return pl.BlockSpec(memory_space=pltpu.VMEM)


def hbm():
    return pl.BlockSpec(memory_space=pltpu.HBM)


def start(pairs, sems):
    copies = [pltpu.make_async_copy(src, dst, sems.at[i]) for i, (src, dst) in enumerate(pairs)]
    for one in copies:
        one.start()
    return copies


def smem():
    return pl.BlockSpec(memory_space=pltpu.SMEM)


def tail_slot(row, q):
    return jnp.where(row == 6, q, jnp.where(row == 7, 3 + q, -1))


def main_slot(row):
    return jnp.where(row < CAP, row, -1)


def prep_kernel(core_ref, routes_ref, weight_ref, tok_ref, go_ref, out_ref, sel_ref, wsel_ref, scale_s):
    picks, rows = routes_ref.shape
    lanes = sel_ref.shape[1]
    half = tok_ref.shape[1] // 2

    @pl.when(pl.program_id(0) == 0)
    def _():
        slot = lax.broadcasted_iota(jnp.int32, (lanes, rows), 0)
        expert, row = slot >> 3, slot & 7
        named = jnp.zeros((lanes, rows), F32)
        weight = jnp.zeros((lanes, rows), F32)
        for k in range(picks):
            hit = routes_ref[k : k + 1, :] == expert
            named = named + jnp.where(hit, 1.0, 0.0)
            weight = weight + jnp.where(hit, weight_ref[k : k + 1, :], 0.0)
        earlier = lax.broadcasted_iota(jnp.int32, (rows, rows), 0) < lax.broadcasted_iota(jnp.int32, (rows, rows), 1)
        before = dot(named.astype(BF16), jnp.where(earlier, 1.0, 0.0).astype(BF16))
        picked, scales = [], []
        for i, want in enumerate([main_slot(row)] + [tail_slot(row, q) for q in range(3)]):
            one = jnp.where((named > 0.5) & (before == want.astype(F32)), 1.0, 0.0)
            sel_ref[i] = one.astype(BF16)
            picked.append(one)
            scales.append(jnp.sum(one * weight, axis=1, keepdims=True))
        plain = jnp.where((lax.broadcasted_iota(jnp.int32, (lanes, 1), 0) & 7) < CAP, 1.0, 0.0)
        scale_s[0] = plain + scales[1]
        scale_s[1] = plain + scales[2]
        scale_s[2] = scales[0] + scales[3]
        wsel = picked[0] * weight
        high = wsel.astype(BF16)
        wsel_ref[0] = high
        wsel_ref[1] = (wsel - high.astype(F32)).astype(BF16)

    own = pl.multiple_of(core_ref[0] * half, 128)
    other = pl.multiple_of((1 - core_ref[0]) * half, 128)
    tail = go_ref[:, pl.ds(other, half)]
    sources = (tok_ref[:, pl.ds(own, half)], tok_ref[:, pl.ds(other, half)], go_ref[:, pl.ds(own, half)])
    tails = dot(sel_ref[1:].reshape(3 * sel_ref.shape[1], sel_ref.shape[2]), tail)
    for q, source in enumerate(sources):
        rows_q = dot(sel_ref[0], source) + tails[q * sel_ref.shape[1] : (q + 1) * sel_ref.shape[1]]
        out_ref[0, :, q * half : (q + 1) * half] = (scale_s[q] * rows_q).astype(BF16)


def prep(core, routes, route_weight, tokens, grad_out, quarters, experts):
    rows, width = tokens.shape
    lanes = experts * PAD
    quarter = width // quarters
    half = quarter // 2
    column = pl.BlockSpec((rows, quarter), lambda i: (0, i))
    return pl.pallas_call(
        prep_kernel,
        grid=(quarters,),
        in_specs=[smem(), whole(), whole(), column, column],
        out_specs=[
            pl.BlockSpec((1, lanes, 3 * half), lambda i: (i, 0, 0)),
            pl.BlockSpec((4, lanes, rows), lambda i: (0, 0, 0)),
            pl.BlockSpec((2, lanes, rows), lambda i: (0, 0, 0)),
        ],
        out_shape=[
            jax.ShapeDtypeStruct((quarters, lanes, 3 * half), BF16),
            jax.ShapeDtypeStruct((4, lanes, rows), BF16),
            jax.ShapeDtypeStruct((2, lanes, rows), BF16),
        ],
        scratch_shapes=[pltpu.VMEM((3, lanes, 1), F32)],
        compiler_params=pltpu.CompilerParams(vmem_limit_bytes=BIG_LIMIT),
        cost_estimate=pl.CostEstimate(flops=800_000_000, bytes_accessed=6_500_000, transcendentals=0),
        name="prep",
    )(core, routes, route_weight, tokens, grad_out)


def slot_masks(slots, lanes, transposed=False):
    shape = (lanes, slots) if transposed else (slots, lanes)
    slot_dim, lane_dim = (1, 0) if transposed else (0, 1)
    slot = lax.broadcasted_iota(jnp.int32, shape, slot_dim)
    lane = lax.broadcasted_iota(jnp.int32, shape, lane_dim)
    expert = (slot * 171) >> 10
    place = slot - expert * CAP
    row = lane & 7
    same = (lane >> 3) == expert
    wants = [main_slot(row)] + [tail_slot(row, q) for q in range(3)]
    return [jnp.where(same & (place == want), 1.0, 0.0).astype(BF16) for want in wants]


def pair_of(ref, p, columns):
    return jnp.concatenate([ref[2 * p, :, columns], ref[2 * p + 1, :, columns]], axis=0)


def share_out(at_ref, total_s, outs):
    quarters = len(outs)
    slots = outs[0].shape[0]
    for j, out in enumerate(outs):
        rows = pl.ds(pl.multiple_of(lax.rem(at_ref[0] + j, quarters) * slots, 32), slots)
        out[...] = total_s[rows, :].astype(out.dtype)


def gate_kernel(at_ref, recv_any, wo_ref, wx_ref, p0_ref, p1_ref, p2_ref, p3_ref, own_ref, other_ref, kept_any, total_s, recv_s, sems):
    quarters, lanes, _ = recv_any.shape
    half = wo_ref.shape[0]
    slots = p0_ref.shape[0]
    pairs = quarters // 2
    copies = start([(recv_any.at[pl.ds(2 * p, 2), :, pl.ds(0, 2 * half)], recv_s.at[p]) for p in range(pairs)], sems)
    main = slot_masks(2 * slots, 2 * lanes)[0]
    for p in range(pairs):
        rows = slice(2 * p * slots, 2 * (p + 1) * slots)
        copies[p].wait()
        block = jnp.concatenate([recv_s[p, 0], recv_s[p, 1]], axis=0)
        own_ref[rows, :] = dot(main, block[:, :half]).astype(BF16)
        other_ref[rows, :] = dot(main, block[:, half:]).astype(BF16)
    total_s[...] = dot(own_ref[...], wo_ref[...]) + dot(other_ref[...], wx_ref[...])
    share_out(at_ref, total_s, (p0_ref, p1_ref, p2_ref, p3_ref))


def up_kernel(at_ref, own_ref, other_ref, wo_ref, wx_ref, p0_ref, p1_ref, p2_ref, p3_ref, total_s):
    total_s[...] = dot(own_ref[...], wo_ref[...]) + dot(other_ref[...], wx_ref[...])
    share_out(at_ref, total_s, (p0_ref, p1_ref, p2_ref, p3_ref))


def back_kernel(at_ref, recv_ref, wo_ref, wx_ref, p0_ref, p1_ref, p2_ref, p3_ref, own_ref, other_ref, total_s):
    quarters, lanes, _ = recv_ref.shape
    half = wo_ref.shape[1]
    slots = p0_ref.shape[0]
    masks = slot_masks(2 * slots, 2 * lanes)
    for p in range(quarters // 2):
        rows = slice(2 * p * slots, 2 * (p + 1) * slots)
        blocks = [pair_of(recv_ref, p, slice(q * half, (q + 1) * half)) for q in range(3)]
        own_ref[rows, :] = dot(masks[0], blocks[2]).astype(BF16)
        other_ref[rows, :] = sum(dot(masks[1 + q], blocks[q]) for q in range(3)).astype(BF16)
    total_s[...] = dot(own_ref[...], wo_ref[...], 1, 1) + dot(other_ref[...], wx_ref[...], 1, 1)
    share_out(at_ref, total_s, (p0_ref, p1_ref, p2_ref, p3_ref))


def projection(kernel, name, at, rows, weights, over, slots, quarters):
    half, hidden = weights[0].shape[over], weights[0].shape[1 - over]
    outs = [jax.ShapeDtypeStruct((slots, hidden), F32 if j == 0 else BF16) for j in range(quarters)]
    scratch = [pltpu.VMEM((quarters * slots, hidden), F32)]
    if len(rows) == 1:
        outs = outs + [jax.ShapeDtypeStruct((quarters * slots, half), BF16)] * 2
    in_specs = [smem()] + [whole()] * (len(rows) + 2)
    out_specs = [whole()] * len(outs)
    aliases = {}
    if kernel is gate_kernel:
        anywhere = pl.BlockSpec(memory_space=pl.ANY)
        in_specs[1] = anywhere
        outs.append(jax.ShapeDtypeStruct(rows[0].shape, BF16))
        out_specs.append(anywhere)
        aliases = {1: len(outs) - 1}
        scratch += [
            pltpu.VMEM((quarters // 2, 2, rows[0].shape[1], 2 * half), BF16),
            pltpu.SemaphoreType.DMA((quarters // 2,)),
        ]
    return pl.pallas_call(
        kernel,
        in_specs=in_specs,
        out_specs=out_specs,
        out_shape=outs,
        scratch_shapes=scratch,
        input_output_aliases=aliases,
        compiler_params=pltpu.CompilerParams(vmem_limit_bytes=VMEM_LIMIT),
        cost_estimate=pl.CostEstimate(flops=3_000_000_000, bytes_accessed=8_000_000, transcendentals=0),
        name=name,
    )(at, *rows, *weights)


def gather_parts(at_ref, parts, all_s):
    quarters = len(parts)
    slots = parts[0].shape[0]
    for j, part in enumerate(parts):
        rows = pl.ds(pl.multiple_of(lax.rem(at_ref[0] + j, quarters) * slots, 32), slots)
        all_s[rows, :] = part[...]


def out_kernel(at_ref, h0, h1, h2, h3, wo_ref, wx_ref, out_ref, all_ref):
    quarters, lanes, width = out_ref.shape
    half = width // 2
    slots = h0.shape[0]
    gather_parts(at_ref, (h0, h1, h2, h3), all_ref)
    main = slot_masks(2 * slots, 2 * lanes, True)[0]
    for q, w_ref in enumerate((wo_ref, wx_ref)):
        value = dot(all_ref[...], w_ref[...]).astype(BF16)
        for p in range(quarters // 2):
            rows = dot(main, value[2 * p * slots : 2 * (p + 1) * slots]).astype(BF16)
            out_ref[2 * p, :, q * half : (q + 1) * half] = rows[:lanes]
            out_ref[2 * p + 1, :, q * half : (q + 1) * half] = rows[lanes:]


def out_rows(at, parts, weights, lanes):
    quarters = len(parts)
    slots, hidden = parts[0].shape
    half = weights[0].shape[1]
    return pl.pallas_call(
        out_kernel,
        in_specs=[smem()] + [whole()] * (quarters + 2),
        out_specs=[whole()] * 2,
        out_shape=[
            jax.ShapeDtypeStruct((quarters, lanes, 2 * half), BF16),
            jax.ShapeDtypeStruct((quarters * slots, hidden), BF16),
        ],
        compiler_params=pltpu.CompilerParams(vmem_limit_bytes=VMEM_LIMIT),
        cost_estimate=pl.CostEstimate(flops=2_000_000_000, bytes_accessed=7_500_000, transcendentals=0),
        name="out_rows",
    )(at, *parts, *weights)


def half_grad_kernel(at_ref, g0, g1, g2, g3, wo_ref, wx_ref, own_ref, other_ref, keep_hbm, all_s, sem):
    gather_parts(at_ref, (g0, g1, g2, g3), all_s)
    keep = pltpu.make_async_copy(all_s, keep_hbm, sem)
    keep.start()
    own_ref[...] = dot(all_s[...], wo_ref[...], 1, 1)
    other_ref[...] = dot(all_s[...], wx_ref[...], 1, 1)
    keep.wait()


def half_grad(at, parts, weights):
    quarters = len(parts)
    slots, hidden = parts[0].shape
    value = jax.ShapeDtypeStruct((quarters * slots, weights[0].shape[0]), F32)
    return pl.pallas_call(
        half_grad_kernel,
        in_specs=[smem()] + [whole()] * (quarters + 2),
        out_specs=[whole(), whole(), hbm()],
        out_shape=[value, value, jax.ShapeDtypeStruct((quarters * slots, hidden), BF16)],
        scratch_shapes=[pltpu.VMEM((quarters * slots, hidden), BF16), pltpu.SemaphoreType.DMA],
        compiler_params=pltpu.CompilerParams(vmem_limit_bytes=SMALL_LIMIT),
        cost_estimate=pl.CostEstimate(flops=1_500_000_000, bytes_accessed=8_000_000, transcendentals=0),
        name="half_grad",
    )(at, *parts, *weights)


def grad_kernel(at_ref, g0, g1, g2, g3, main_ref, half_own_ref, half_other_ref, wo_ref, wx_ref, out_ref, keep_hbm, all_s, sem):
    quarters, lanes, packed = out_ref.shape
    half = packed // 3
    slots = g0.shape[0]
    gather_parts(at_ref, (g0, g1, g2, g3), all_s)
    keep = pltpu.make_async_copy(all_s, keep_hbm, sem)
    keep.start()
    masks = slot_masks(2 * slots, 2 * lanes, True)
    tail_masks = jnp.concatenate(masks[1:], axis=0)
    other = (half_other_ref[...] + dot(all_s[...], wx_ref[...], 1, 1)).astype(BF16)
    own = (half_own_ref[...] + dot(all_s[...], wo_ref[...], 1, 1)).astype(BF16)
    for p in range(quarters // 2):
        rows = slice(2 * p * slots, 2 * (p + 1) * slots)
        tails = dot(tail_masks, other[rows])
        for q in range(3):
            columns = slice(q * half, (q + 1) * half)
            value = tails[2 * q * lanes : 2 * (q + 1) * lanes]
            if q == 2:
                value = value + dot(masks[0], own[rows])
            else:
                mine = jnp.concatenate([main_ref[2 * p, :, columns], main_ref[2 * p + 1, :, columns]], axis=0)
                value = value + mine.astype(F32)
            value = value.astype(BF16)
            out_ref[2 * p, :, columns] = value[:lanes]
            out_ref[2 * p + 1, :, columns] = value[lanes:]
    keep.wait()


def grad_rows(at, parts, main, halves, weights):
    quarters, lanes, width = main.shape
    slots, hidden = parts[0].shape
    return pl.pallas_call(
        grad_kernel,
        in_specs=[smem()] + [whole()] * (quarters + 5),
        out_specs=[whole(), hbm()],
        out_shape=[
            jax.ShapeDtypeStruct((quarters, lanes, width // 2 * 3), BF16),
            jax.ShapeDtypeStruct((quarters * slots, hidden), BF16),
        ],
        scratch_shapes=[pltpu.VMEM((quarters * slots, hidden), BF16), pltpu.SemaphoreType.DMA],
        compiler_params=pltpu.CompilerParams(vmem_limit_bytes=SMALL_LIMIT),
        cost_estimate=pl.CostEstimate(flops=2_500_000_000, bytes_accessed=14_000_000, transcendentals=0),
        name="grad_rows",
    )(at, *parts, main, *halves, *weights)


def weight_kernel(am_ref, ap_ref, bm_ref, bp_ref, out_ref):
    out_ref[...] = (dot(am_ref[...], bm_ref[...], 0, 0) + dot(ap_ref[...], bp_ref[...], 0, 0)).astype(BF16)


def weight_grad(a_mine, a_partner, b_mine, b_partner, step, at=0, columns=None):
    slots, rows = a_mine.shape
    columns = columns or b_mine.shape[1]
    a_spec = pl.BlockSpec((slots, rows), lambda n: (0, 0))
    b_spec = pl.BlockSpec((slots, step), lambda n: (0, n + at))
    return pl.pallas_call(
        weight_kernel,
        grid=(columns // step,),
        in_specs=[a_spec, a_spec, b_spec, b_spec],
        out_specs=pl.BlockSpec((rows, step), lambda n: (0, n)),
        out_shape=jax.ShapeDtypeStruct((rows, columns), BF16),
        compiler_params=pltpu.CompilerParams(vmem_limit_bytes=VMEM_LIMIT),
        cost_estimate=pl.CostEstimate(flops=1_500_000_000, bytes_accessed=5_000_000, transcendentals=0),
        name="weight_grad",
    )(a_mine, a_partner, b_mine, b_partner)


def last_kernel(core_ref, routes_ref, sel_ref, wsel_ref, recv_ref, go_ref, moe_ref, gt_ref, gr_ref, inner_s, lhs_s):
    step = pl.program_id(0)
    half = go_ref.shape[1] // 2
    own = pl.ds(pl.multiple_of(core_ref[0] * half, 128), half)
    other = pl.ds(pl.multiple_of((1 - core_ref[0]) * half, 128), half)
    block = [recv_ref[0, :, q * half : (q + 1) * half] for q in range(3)]
    rows = go_ref.shape[0]

    @pl.when(step == 0)
    def _():
        for q in range(2):
            for i, one in enumerate((wsel_ref[0], wsel_ref[1], sel_ref[1 + q])):
                lhs_s[q, i * rows : (i + 1) * rows, :] = one.astype(F32).T.astype(BF16)
        for i in (0, 3):
            lhs_s[2, i // 3 * rows : (i // 3 + 1) * rows, :] = sel_ref[i].astype(F32).T.astype(BF16)

    first, second, third = dot(lhs_s[0], block[0]), dot(lhs_s[1], block[1]), dot(lhs_s[2, : 2 * rows, :], block[2])
    moe_ref[:, own] = (first[:rows] + first[rows : 2 * rows]).astype(BF16)
    moe_ref[:, other] = (second[:rows] + second[rows : 2 * rows]).astype(BF16)
    gt_ref[:, own] = third[:rows].astype(BF16)
    gt_ref[:, other] = (first[2 * rows :] + second[2 * rows :] + third[rows:]).astype(BF16)
    inner = dot(block[0], go_ref[:, own], 1, 1) + dot(block[1], go_ref[:, other], 1, 1)

    @pl.when(step == 0)
    def _():
        inner_s[...] = inner

    @pl.when(step > 0)
    def _():
        inner_s[...] += inner

    @pl.when(step == pl.num_programs(0) - 1)
    def _():
        picks, rows = routes_ref.shape
        lanes = sel_ref.shape[1]
        expert = lax.broadcasted_iota(jnp.int32, (lanes, rows), 0) >> 3
        held = sel_ref[0].astype(F32) * inner_s[...]
        for k in range(picks):
            mine = jnp.where(routes_ref[k : k + 1, :] == expert, held, 0.0)
            gr_ref[k : k + 1, :] = jnp.sum(mine, axis=0, keepdims=True)


def last(core, routes, sel, wsel, recv, grad_out):
    rows, width = grad_out.shape
    quarters, lanes, packed = recv.shape
    column = pl.BlockSpec((rows, width // quarters), lambda i: (0, i))
    return pl.pallas_call(
        last_kernel,
        grid=(quarters,),
        in_specs=[smem(), whole(), whole(), whole(), pl.BlockSpec((1, lanes, packed), lambda i: (i, 0, 0)), column],
        out_specs=[column, column, pl.BlockSpec(routes.shape, lambda i: (0, 0))],
        out_shape=[
            jax.ShapeDtypeStruct((rows, width), BF16),
            jax.ShapeDtypeStruct((rows, width), BF16),
            jax.ShapeDtypeStruct(routes.shape, F32),
        ],
        scratch_shapes=[pltpu.VMEM((lanes, rows), F32), pltpu.VMEM((3, 3 * rows, lanes), BF16)],
        compiler_params=pltpu.CompilerParams(vmem_limit_bytes=BIG_LIMIT),
        cost_estimate=pl.CostEstimate(flops=1_500_000_000, bytes_accessed=8_500_000, transcendentals=0),
        name="last",
    )(core, routes, sel, wsel, recv, grad_out)


def on_device(tokens, routes, route_weight, w_gate, w_up, w_down, grad_out):
    quarters = lax.axis_size("y")
    experts = lax.axis_size("x") * lax.axis_size("z")
    slots = experts * CAP
    lanes = experts * PAD
    hidden = w_gate.shape[2]
    everyone = ("y", "x", "z")
    half = w_gate.shape[1]
    core = lax.axis_index("k").astype(jnp.int32).reshape(1)
    at = lax.axis_index("y").astype(jnp.int32).reshape(1)

    def to_partner(value):
        return lax.ppermute(value, "k", [(0, 1), (1, 0)])

    def along(value, shift):
        return lax.ppermute(value, "y", [(i, (i + shift) % quarters) for i in range(quarters)])

    def exchange(value):
        flat = value.reshape(quarters * experts, PAD, value.shape[2])
        return lax.all_to_all(flat, everyone, 0, 0, tiled=True).reshape(value.shape)

    def add_over_y(shares):
        total = shares[0]
        for j in (2, 1, 3):
            total = total + along(shares[j], j).astype(F32)
        return total

    def from_y(value):
        return [value] + [along(value, quarters - j) for j in range(1, quarters)]

    gate_own, up_own, down_own = w_gate[0], w_up[0], w_down[0]
    gate_other, up_other, down_other = to_partner(gate_own), to_partner(up_own), to_partner(down_own)
    routes, route_weight = routes.T, route_weight.T

    sent, sel, wsel = prep(core, routes, route_weight, tokens, grad_out, quarters, experts)
    recv = exchange(sent)
    down = (down_own, down_other)
    *shares, x_own, x_other, recv = projection(gate_kernel, "gate", at, (recv,), (gate_own, gate_other), 0, slots, quarters)
    gate = add_over_y(shares)
    shares = projection(up_kernel, "up", at, (x_own, x_other), (up_own, up_other), 0, slots, quarters)
    up = add_over_y(shares)
    *shares, d_own, d_other = projection(back_kernel, "back", at, (recv,), down, 1, slots, quarters)
    back = add_over_y(shares)

    sig = jax.nn.sigmoid(gate)
    smooth = gate * sig
    slope = up * (sig * (1.0 + gate * (1.0 - sig)))
    mine, smooth, slope = lax.optimization_barrier(((smooth * up).astype(BF16), smooth, slope))
    h_parts = from_y(mine)
    back, h_parts = lax.optimization_barrier((back, h_parts))
    dg_parts = from_y((back * slope).astype(BF16))
    main, h_mine = out_rows(at, h_parts, down, lanes)
    du, main = lax.optimization_barrier(((back * smooth).astype(BF16), main))
    du_parts = from_y(du)
    *halves, dg_mine = half_grad(at, dg_parts, (gate_own, gate_other))
    packed, du_mine = grad_rows(at, du_parts, main, halves, (up_own, up_other))
    x_other, d_other, h_mine, dg_mine, du_mine = lax.optimization_barrier((x_other, d_other, h_mine, dg_mine, du_mine))
    returned = exchange(packed)

    x_partner, d_partner, h_partner = to_partner(x_other), to_partner(d_other), to_partner(h_mine)
    dg_partner, du_partner = to_partner(dg_mine), to_partner(du_mine)
    step = hidden // 4
    grad_down = weight_grad(h_mine, h_partner, d_own, d_partner, half)
    grad_gate = weight_grad(x_own, x_partner, dg_mine, dg_partner, step)
    grad_up = weight_grad(x_own, x_partner, du_mine, du_partner, step)
    returned, grad_gate, grad_up, grad_down = lax.optimization_barrier((returned, grad_gate, grad_up, grad_down))

    moe_out, grad_tokens, grad_route = last(core, routes, sel, wsel, returned, grad_out)
    return (moe_out, grad_tokens, grad_route.T, grad_gate[None], grad_up[None], grad_down[None])


def solution(mesh):
    ctx, head = mesh.shape["ctx"], mesh.shape["head"]
    side = int(round(ctx**0.5))
    fine = Mesh(mesh.devices.reshape(side, ctx // side, head // 2, 2), ("x", "z", "y", "k"))
    e, d, both = ("x", "z"), ("y", "k"), ("x", "z", "y", "k")
    rows = P(both, None)
    up, down = P(e, d, None), P(e, None, d)
    return jax.shard_map(
        on_device,
        mesh=fine,
        in_specs=(rows, rows, rows, up, up, down, rows),
        out_specs=(rows, rows, rows, up, up, down),
        check_vma=False,
    )
```

```python
import functools

import jax
import jax.numpy as jnp
from jax import lax
from jax.experimental import pallas as pl
from jax.experimental.pallas import tpu as pltpu
from jax.sharding import Mesh, PartitionSpec as P

CAP = 6
PAD = 8
BF16 = jnp.bfloat16
F32 = jnp.float32
VMEM_LIMIT = 32 * 1024 * 1024
SMALL_LIMIT = 32 * 1024 * 1024
BIG_LIMIT = 60 * 1024 * 1024


def dot(a, b, ca=1, cb=0):
    return lax.dot_general(a, b, (((ca,), (cb,)), ((), ())), preferred_element_type=F32)


def whole():
    return pl.BlockSpec(memory_space=pltpu.VMEM)


def hbm():
    return pl.BlockSpec(memory_space=pltpu.HBM)


def start(pairs, sems):
    copies = [pltpu.make_async_copy(src, dst, sems.at[i]) for i, (src, dst) in enumerate(pairs)]
    for one in copies:
        one.start()
    return copies


def smem():
    return pl.BlockSpec(memory_space=pltpu.SMEM)


def tail_slot(row, q):
    return jnp.where(row == 6, q, jnp.where(row == 7, 3 + q, -1))


def main_slot(row):
    return jnp.where(row < CAP, row, -1)


def prep_kernel(core_ref, routes_ref, weight_ref, tok_ref, go_ref, out_ref, sel_ref, wsel_ref, scale_s):
    picks, rows = routes_ref.shape
    lanes = sel_ref.shape[1]
    half = tok_ref.shape[1] // 2

    @pl.when(pl.program_id(0) == 0)
    def _():
        slot = lax.broadcasted_iota(jnp.int32, (lanes, rows), 0)
        expert, row = slot >> 3, slot & 7
        named = jnp.zeros((lanes, rows), F32)
        weight = jnp.zeros((lanes, rows), F32)
        for k in range(picks):
            hit = routes_ref[k : k + 1, :] == expert
            named = named + jnp.where(hit, 1.0, 0.0)
            weight = weight + jnp.where(hit, weight_ref[k : k + 1, :], 0.0)
        earlier = lax.broadcasted_iota(jnp.int32, (rows, rows), 0) < lax.broadcasted_iota(jnp.int32, (rows, rows), 1)
        before = dot(named.astype(BF16), jnp.where(earlier, 1.0, 0.0).astype(BF16))
        picked, scales = [], []
        for i, want in enumerate([main_slot(row)] + [tail_slot(row, q) for q in range(3)]):
            one = jnp.where((named > 0.5) & (before == want.astype(F32)), 1.0, 0.0)
            sel_ref[i] = one.astype(BF16)
            picked.append(one)
            scales.append(jnp.sum(one * weight, axis=1, keepdims=True))
        plain = jnp.where((lax.broadcasted_iota(jnp.int32, (lanes, 1), 0) & 7) < CAP, 1.0, 0.0)
        scale_s[0] = plain + scales[1]
        scale_s[1] = plain + scales[2]
        scale_s[2] = scales[0] + scales[3]
        wsel = picked[0] * weight
        high = wsel.astype(BF16)
        wsel_ref[0] = high
        wsel_ref[1] = (wsel - high.astype(F32)).astype(BF16)

    own = pl.multiple_of(core_ref[0] * half, 128)
    other = pl.multiple_of((1 - core_ref[0]) * half, 128)
    tail = go_ref[:, pl.ds(other, half)]
    sources = (tok_ref[:, pl.ds(own, half)], tok_ref[:, pl.ds(other, half)], go_ref[:, pl.ds(own, half)])
    tails = dot(sel_ref[1:].reshape(3 * sel_ref.shape[1], sel_ref.shape[2]), tail)
    for q, source in enumerate(sources):
        rows_q = dot(sel_ref[0], source) + tails[q * sel_ref.shape[1] : (q + 1) * sel_ref.shape[1]]
        out_ref[0, :, q * half : (q + 1) * half] = (scale_s[q] * rows_q).astype(BF16)


def prep(core, routes, route_weight, tokens, grad_out, quarters, experts):
    rows, width = tokens.shape
    lanes = experts * PAD
    quarter = width // quarters
    half = quarter // 2
    column = pl.BlockSpec((rows, quarter), lambda i: (0, i))
    return pl.pallas_call(
        prep_kernel,
        grid=(quarters,),
        in_specs=[smem(), whole(), whole(), column, column],
        out_specs=[
            pl.BlockSpec((1, lanes, 3 * half), lambda i: (i, 0, 0)),
            pl.BlockSpec((4, lanes, rows), lambda i: (0, 0, 0)),
            pl.BlockSpec((2, lanes, rows), lambda i: (0, 0, 0)),
        ],
        out_shape=[
            jax.ShapeDtypeStruct((quarters, lanes, 3 * half), BF16),
            jax.ShapeDtypeStruct((4, lanes, rows), BF16),
            jax.ShapeDtypeStruct((2, lanes, rows), BF16),
        ],
        scratch_shapes=[pltpu.VMEM((3, lanes, 1), F32)],
        compiler_params=pltpu.CompilerParams(vmem_limit_bytes=BIG_LIMIT),
        cost_estimate=pl.CostEstimate(flops=800_000_000, bytes_accessed=6_500_000, transcendentals=0),
        name="prep",
    )(core, routes, route_weight, tokens, grad_out)


def slot_masks(slots, lanes, transposed=False):
    shape = (lanes, slots) if transposed else (slots, lanes)
    slot_dim, lane_dim = (1, 0) if transposed else (0, 1)
    slot = lax.broadcasted_iota(jnp.int32, shape, slot_dim)
    lane = lax.broadcasted_iota(jnp.int32, shape, lane_dim)
    expert = (slot * 171) >> 10
    place = slot - expert * CAP
    row = lane & 7
    same = (lane >> 3) == expert
    wants = [main_slot(row)] + [tail_slot(row, q) for q in range(3)]
    return [jnp.where(same & (place == want), 1.0, 0.0).astype(BF16) for want in wants]


def pair_of(ref, p, columns):
    return jnp.concatenate([ref[2 * p, :, columns], ref[2 * p + 1, :, columns]], axis=0)


def share_out(at_ref, total_s, outs):
    quarters = len(outs)
    slots = outs[0].shape[0]
    for j, out in enumerate(outs):
        rows = pl.ds(pl.multiple_of(lax.rem(at_ref[0] + j, quarters) * slots, 32), slots)
        out[...] = total_s[rows, :].astype(out.dtype)


def unpack_kernel(recv_any, wx_ref, own_ref, other_ref, total_ref, _, recv_s, sems):
    quarters, lanes, _ = recv_any.shape
    half = own_ref.shape[1]
    slots = own_ref.shape[0] // quarters
    pairs = quarters // 2
    copies = start([(recv_any.at[pl.ds(2 * p, 2), :, pl.ds(0, 2 * half)], recv_s.at[p]) for p in range(pairs)], sems)
    main = slot_masks(2 * slots, 2 * lanes)[0]
    for p in range(pairs):
        rows = slice(2 * p * slots, 2 * (p + 1) * slots)
        copies[p].wait()
        block = jnp.concatenate([recv_s[p, 0], recv_s[p, 1]], axis=0)
        own_ref[rows, :] = dot(main, block[:, :half]).astype(BF16)
        other_ref[rows, :] = dot(main, block[:, half:]).astype(BF16)
    total_ref[...] = dot(other_ref[...], wx_ref[...])


def unpack_x(recv, other_weight, slots):
    quarters, lanes, _ = recv.shape
    half, hidden = other_weight.shape
    anywhere = pl.BlockSpec(memory_space=pl.ANY)
    rows = jax.ShapeDtypeStruct((quarters * slots, half), BF16)
    return pl.pallas_call(
        unpack_kernel,
        in_specs=[anywhere, whole()],
        out_specs=[whole()] * 3 + [anywhere],
        out_shape=[
            rows,
            rows,
            jax.ShapeDtypeStruct((quarters * slots, hidden), F32),
            jax.ShapeDtypeStruct(recv.shape, BF16),
        ],
        scratch_shapes=[
            pltpu.VMEM((quarters // 2, 2, lanes, 2 * half), BF16),
            pltpu.SemaphoreType.DMA((quarters // 2,)),
        ],
        input_output_aliases={0: 3},
        compiler_params=pltpu.CompilerParams(vmem_limit_bytes=VMEM_LIMIT),
        cost_estimate=pl.CostEstimate(flops=2_000_000_000, bytes_accessed=6_000_000, transcendentals=0),
        name="unpack_x",
    )(recv, other_weight)


def gate_kernel(at_ref, own_ref, part_ref, wo_ref, p0_ref, p1_ref, p2_ref, p3_ref, total_s):
    total_s[...] = part_ref[...] + dot(own_ref[...], wo_ref[...])
    share_out(at_ref, total_s, (p0_ref, p1_ref, p2_ref, p3_ref))


def up_kernel(at_ref, own_ref, other_ref, wo_ref, wx_ref, p0_ref, p1_ref, p2_ref, p3_ref, total_s):
    total_s[...] = dot(own_ref[...], wo_ref[...]) + dot(other_ref[...], wx_ref[...])
    share_out(at_ref, total_s, (p0_ref, p1_ref, p2_ref, p3_ref))


def back_kernel(at_ref, recv_ref, wo_ref, wx_ref, p0_ref, p1_ref, p2_ref, p3_ref, own_ref, other_ref, total_s):
    quarters, lanes, _ = recv_ref.shape
    half = wo_ref.shape[1]
    slots = p0_ref.shape[0]
    masks = slot_masks(2 * slots, 2 * lanes)
    for p in range(quarters // 2):
        rows = slice(2 * p * slots, 2 * (p + 1) * slots)
        blocks = [pair_of(recv_ref, p, slice(q * half, (q + 1) * half)) for q in range(3)]
        own_ref[rows, :] = dot(masks[0], blocks[2]).astype(BF16)
        other_ref[rows, :] = sum(dot(masks[1 + q], blocks[q]) for q in range(3)).astype(BF16)
    total_s[...] = dot(own_ref[...], wo_ref[...], 1, 1) + dot(other_ref[...], wx_ref[...], 1, 1)
    share_out(at_ref, total_s, (p0_ref, p1_ref, p2_ref, p3_ref))


def projection(kernel, name, at, rows, weights, over, slots, quarters):
    half, hidden = weights[0].shape[over], weights[0].shape[1 - over]
    outs = [jax.ShapeDtypeStruct((slots, hidden), F32 if j == 0 else BF16) for j in range(quarters)]
    if len(rows) == 1:
        outs = outs + [jax.ShapeDtypeStruct((quarters * slots, half), BF16)] * 2
    return pl.pallas_call(
        kernel,
        in_specs=[smem()] + [whole()] * (len(rows) + len(weights)),
        out_specs=[whole()] * len(outs),
        out_shape=outs,
        scratch_shapes=[pltpu.VMEM((quarters * slots, hidden), F32)],
        compiler_params=pltpu.CompilerParams(vmem_limit_bytes=VMEM_LIMIT),
        cost_estimate=pl.CostEstimate(flops=3_000_000_000, bytes_accessed=8_000_000, transcendentals=0),
        name=name,
    )(at, *rows, *weights)


def gather_parts(at_ref, parts, all_s):
    quarters = len(parts)
    slots = parts[0].shape[0]
    for j, part in enumerate(parts):
        rows = pl.ds(pl.multiple_of(lax.rem(at_ref[0] + j, quarters) * slots, 32), slots)
        all_s[rows, :] = part[...]


def out_kernel(at_ref, h0, h1, h2, h3, wo_ref, wx_ref, out_ref, all_ref):
    quarters, lanes, width = out_ref.shape
    half = width // 2
    slots = h0.shape[0]
    gather_parts(at_ref, (h0, h1, h2, h3), all_ref)
    main = slot_masks(2 * slots, 2 * lanes, True)[0]
    for q, w_ref in enumerate((wo_ref, wx_ref)):
        value = dot(all_ref[...], w_ref[...]).astype(BF16)
        for p in range(quarters // 2):
            rows = dot(main, value[2 * p * slots : 2 * (p + 1) * slots]).astype(BF16)
            out_ref[2 * p, :, q * half : (q + 1) * half] = rows[:lanes]
            out_ref[2 * p + 1, :, q * half : (q + 1) * half] = rows[lanes:]


def out_rows(at, parts, weights, lanes):
    quarters = len(parts)
    slots, hidden = parts[0].shape
    half = weights[0].shape[1]
    return pl.pallas_call(
        out_kernel,
        in_specs=[smem()] + [whole()] * (quarters + 2),
        out_specs=[whole()] * 2,
        out_shape=[
            jax.ShapeDtypeStruct((quarters, lanes, 2 * half), BF16),
            jax.ShapeDtypeStruct((quarters * slots, hidden), BF16),
        ],
        compiler_params=pltpu.CompilerParams(vmem_limit_bytes=VMEM_LIMIT),
        cost_estimate=pl.CostEstimate(flops=2_000_000_000, bytes_accessed=7_500_000, transcendentals=0),
        name="out_rows",
    )(at, *parts, *weights)


def half_grad_kernel(at_ref, g0, g1, g2, g3, wo_ref, wx_ref, own_ref, other_ref, keep_hbm, all_s, sem):
    gather_parts(at_ref, (g0, g1, g2, g3), all_s)
    keep = pltpu.make_async_copy(all_s, keep_hbm, sem)
    keep.start()
    own_ref[...] = dot(all_s[...], wo_ref[...], 1, 1)
    other_ref[...] = dot(all_s[...], wx_ref[...], 1, 1)
    keep.wait()


def half_grad(at, parts, weights):
    quarters = len(parts)
    slots, hidden = parts[0].shape
    value = jax.ShapeDtypeStruct((quarters * slots, weights[0].shape[0]), F32)
    return pl.pallas_call(
        half_grad_kernel,
        in_specs=[smem()] + [whole()] * (quarters + 2),
        out_specs=[whole(), whole(), hbm()],
        out_shape=[value, value, jax.ShapeDtypeStruct((quarters * slots, hidden), BF16)],
        scratch_shapes=[pltpu.VMEM((quarters * slots, hidden), BF16), pltpu.SemaphoreType.DMA],
        compiler_params=pltpu.CompilerParams(vmem_limit_bytes=SMALL_LIMIT),
        cost_estimate=pl.CostEstimate(flops=1_500_000_000, bytes_accessed=8_000_000, transcendentals=0),
        name="half_grad",
    )(at, *parts, *weights)


def grad_kernel(at_ref, g0, g1, g2, g3, main_ref, half_own_ref, half_other_ref, wo_ref, wx_ref, out_ref, keep_hbm, all_s, sem):
    quarters, lanes, packed = out_ref.shape
    half = packed // 3
    slots = g0.shape[0]
    gather_parts(at_ref, (g0, g1, g2, g3), all_s)
    keep = pltpu.make_async_copy(all_s, keep_hbm, sem)
    keep.start()
    masks = slot_masks(2 * slots, 2 * lanes, True)
    tail_masks = jnp.concatenate(masks[1:], axis=0)
    other = (half_other_ref[...] + dot(all_s[...], wx_ref[...], 1, 1)).astype(BF16)
    own = (half_own_ref[...] + dot(all_s[...], wo_ref[...], 1, 1)).astype(BF16)
    for p in range(quarters // 2):
        rows = slice(2 * p * slots, 2 * (p + 1) * slots)
        tails = dot(tail_masks, other[rows])
        for q in range(3):
            columns = slice(q * half, (q + 1) * half)
            value = tails[2 * q * lanes : 2 * (q + 1) * lanes]
            if q == 2:
                value = value + dot(masks[0], own[rows])
            for i in range(2):
                part = value[i * lanes : (i + 1) * lanes].astype(BF16)
                out_ref[2 * p + i, :, columns] = part if q == 2 else part + main_ref[2 * p + i, :, columns]
    keep.wait()


def grad_rows(at, parts, main, halves, weights):
    quarters, lanes, width = main.shape
    slots, hidden = parts[0].shape
    return pl.pallas_call(
        grad_kernel,
        in_specs=[smem()] + [whole()] * (quarters + 5),
        out_specs=[whole(), hbm()],
        out_shape=[
            jax.ShapeDtypeStruct((quarters, lanes, width // 2 * 3), BF16),
            jax.ShapeDtypeStruct((quarters * slots, hidden), BF16),
        ],
        scratch_shapes=[pltpu.VMEM((quarters * slots, hidden), BF16), pltpu.SemaphoreType.DMA],
        compiler_params=pltpu.CompilerParams(vmem_limit_bytes=SMALL_LIMIT),
        cost_estimate=pl.CostEstimate(flops=2_500_000_000, bytes_accessed=14_000_000, transcendentals=0),
        name="grad_rows",
    )(at, *parts, main, *halves, *weights)


def weight_kernel(am_ref, ap_ref, bm_ref, bp_ref, out_ref):
    out_ref[...] = (dot(am_ref[...], bm_ref[...], 0, 0) + dot(ap_ref[...], bp_ref[...], 0, 0)).astype(BF16)


def weight_grad(a_mine, a_partner, b_mine, b_partner, step, at=0, columns=None):
    slots, rows = a_mine.shape
    columns = columns or b_mine.shape[1]
    a_spec = pl.BlockSpec((slots, rows), lambda n: (0, 0))
    b_spec = pl.BlockSpec((slots, step), lambda n: (0, n + at))
    return pl.pallas_call(
        weight_kernel,
        grid=(columns // step,),
        in_specs=[a_spec, a_spec, b_spec, b_spec],
        out_specs=pl.BlockSpec((rows, step), lambda n: (0, n)),
        out_shape=jax.ShapeDtypeStruct((rows, columns), BF16),
        compiler_params=pltpu.CompilerParams(vmem_limit_bytes=VMEM_LIMIT),
        cost_estimate=pl.CostEstimate(flops=1_500_000_000, bytes_accessed=5_000_000, transcendentals=0),
        name="weight_grad",
    )(a_mine, a_partner, b_mine, b_partner)


def last_kernel(core_ref, routes_ref, sel_ref, wsel_ref, recv_ref, go_ref, moe_ref, gt_ref, gr_ref, inner_s, lhs_s):
    step = pl.program_id(0)
    half = go_ref.shape[1] // 2
    own = pl.ds(pl.multiple_of(core_ref[0] * half, 128), half)
    other = pl.ds(pl.multiple_of((1 - core_ref[0]) * half, 128), half)
    block = [recv_ref[0, :, q * half : (q + 1) * half] for q in range(3)]
    rows = go_ref.shape[0]

    @pl.when(step == 0)
    def _():
        for q in range(2):
            for i, one in enumerate((wsel_ref[0], wsel_ref[1], sel_ref[1 + q])):
                lhs_s[q, i * rows : (i + 1) * rows, :] = one.astype(F32).T.astype(BF16)
        for i in (0, 3):
            lhs_s[2, i // 3 * rows : (i // 3 + 1) * rows, :] = sel_ref[i].astype(F32).T.astype(BF16)

    first, second, third = dot(lhs_s[0], block[0]), dot(lhs_s[1], block[1]), dot(lhs_s[2, : 2 * rows, :], block[2])
    moe_ref[:, own] = (first[:rows] + first[rows : 2 * rows]).astype(BF16)
    moe_ref[:, other] = (second[:rows] + second[rows : 2 * rows]).astype(BF16)
    gt_ref[:, own] = third[:rows].astype(BF16)
    gt_ref[:, other] = (first[2 * rows :] + second[2 * rows :] + third[rows:]).astype(BF16)
    inner = dot(block[0], go_ref[:, own], 1, 1) + dot(block[1], go_ref[:, other], 1, 1)

    @pl.when(step == 0)
    def _():
        inner_s[...] = inner

    @pl.when(step > 0)
    def _():
        inner_s[...] += inner

    @pl.when(step == pl.num_programs(0) - 1)
    def _():
        picks, rows = routes_ref.shape
        lanes = sel_ref.shape[1]
        expert = lax.broadcasted_iota(jnp.int32, (lanes, rows), 0) >> 3
        held = sel_ref[0].astype(F32) * inner_s[...]
        for k in range(picks):
            mine = jnp.where(routes_ref[k : k + 1, :] == expert, held, 0.0)
            gr_ref[k : k + 1, :] = jnp.sum(mine, axis=0, keepdims=True)


def last(core, routes, sel, wsel, recv, grad_out):
    rows, width = grad_out.shape
    quarters, lanes, packed = recv.shape
    column = pl.BlockSpec((rows, width // quarters), lambda i: (0, i))
    return pl.pallas_call(
        last_kernel,
        grid=(quarters,),
        in_specs=[smem(), whole(), whole(), whole(), pl.BlockSpec((1, lanes, packed), lambda i: (i, 0, 0)), column],
        out_specs=[column, column, pl.BlockSpec(routes.shape, lambda i: (0, 0))],
        out_shape=[
            jax.ShapeDtypeStruct((rows, width), BF16),
            jax.ShapeDtypeStruct((rows, width), BF16),
            jax.ShapeDtypeStruct(routes.shape, F32),
        ],
        scratch_shapes=[pltpu.VMEM((lanes, rows), F32), pltpu.VMEM((3, 3 * rows, lanes), BF16)],
        compiler_params=pltpu.CompilerParams(vmem_limit_bytes=BIG_LIMIT),
        cost_estimate=pl.CostEstimate(flops=1_500_000_000, bytes_accessed=8_500_000, transcendentals=0),
        name="last",
    )(core, routes, sel, wsel, recv, grad_out)


def on_device(tokens, routes, route_weight, w_gate, w_up, w_down, grad_out):
    quarters = lax.axis_size("y")
    experts = lax.axis_size("x") * lax.axis_size("z")
    slots = experts * CAP
    lanes = experts * PAD
    hidden = w_gate.shape[2]
    everyone = ("y", "x", "z")
    half = w_gate.shape[1]
    core = lax.axis_index("k").astype(jnp.int32).reshape(1)
    at = lax.axis_index("y").astype(jnp.int32).reshape(1)

    def to_partner(value):
        return lax.ppermute(value, "k", [(0, 1), (1, 0)])

    def along(value, shift):
        return lax.ppermute(value, "y", [(i, (i + shift) % quarters) for i in range(quarters)])

    def exchange(value):
        flat = value.reshape(quarters * experts, PAD, value.shape[2])
        return lax.all_to_all(flat, everyone, 0, 0, tiled=True).reshape(value.shape)

    def add_over_y(shares):
        total = shares[0]
        for j in (2, 1, 3):
            total = total + along(shares[j], j).astype(F32)
        return total

    def from_y(value):
        got = {j: along(value, quarters - j) for j in (2, 1, 3)}
        return [value, got[1], got[2], got[3]]

    gate_own, up_own, down_own = w_gate[0], w_up[0], w_down[0]
    gate_other, up_other, down_other = to_partner(gate_own), to_partner(up_own), to_partner(down_own)
    routes, route_weight = routes.T, route_weight.T

    sent, sel, wsel = prep(core, routes, route_weight, tokens, grad_out, quarters, experts)
    recv = exchange(sent)
    down = (down_own, down_other)
    x_own, x_other, part, recv = unpack_x(recv, gate_other, slots)
    gate = add_over_y(projection(gate_kernel, "gate", at, (x_own, part), (gate_own,), 0, slots, quarters))
    shares = projection(up_kernel, "up", at, (x_own, x_other), (up_own, up_other), 0, slots, quarters)
    up = add_over_y(shares)
    *shares, d_own, d_other = projection(back_kernel, "back", at, (recv,), down, 1, slots, quarters)
    back = add_over_y(shares)

    sig = jax.nn.sigmoid(gate)
    smooth = gate * sig
    slope = up * (sig * (1.0 + gate * (1.0 - sig)))
    mine, smooth, slope = lax.optimization_barrier(((smooth * up).astype(BF16), smooth, slope))
    h_parts = from_y(mine)
    back, h_parts = lax.optimization_barrier((back, h_parts))
    dg_parts = from_y((back * slope).astype(BF16))
    main, h_mine = out_rows(at, h_parts, down, lanes)
    du, main = lax.optimization_barrier(((back * smooth).astype(BF16), main))
    du_parts = from_y(du)
    *halves, dg_mine = half_grad(at, dg_parts, (gate_own, gate_other))
    packed, du_mine = grad_rows(at, du_parts, main, halves, (up_own, up_other))
    x_other, d_other, h_mine, dg_mine, du_mine = lax.optimization_barrier((x_other, d_other, h_mine, dg_mine, du_mine))
    returned = exchange(packed)

    x_partner, d_partner, h_partner = to_partner(x_other), to_partner(d_other), to_partner(h_mine)
    dg_partner, du_partner = to_partner(dg_mine), to_partner(du_mine)
    step = hidden // 4
    grad_down = weight_grad(h_mine, h_partner, d_own, d_partner, half)
    grad_gate = weight_grad(x_own, x_partner, dg_mine, dg_partner, step)
    grad_up = weight_grad(x_own, x_partner, du_mine, du_partner, step)
    returned, grad_gate, grad_up, grad_down = lax.optimization_barrier((returned, grad_gate, grad_up, grad_down))

    moe_out, grad_tokens, grad_route = last(core, routes, sel, wsel, returned, grad_out)
    return (moe_out, grad_tokens, grad_route.T, grad_gate[None], grad_up[None], grad_down[None])


def solution(mesh):
    ctx, head = mesh.shape["ctx"], mesh.shape["head"]
    side = int(round(ctx**0.5))
    fine = Mesh(mesh.devices.reshape(side, ctx // side, head // 2, 2), ("x", "z", "y", "k"))
    e, d, both = ("x", "z"), ("y", "k"), ("x", "z", "y", "k")
    rows = P(both, None)
    up, down = P(e, d, None), P(e, None, d)
    return jax.shard_map(
        on_device,
        mesh=fine,
        in_specs=(rows, rows, rows, up, up, down, rows),
        out_specs=(rows, rows, rows, up, up, down),
        check_vma=False,
    )
```

```python
import functools

import jax
import jax.numpy as jnp
from jax import lax
from jax.experimental import pallas as pl
from jax.experimental.pallas import tpu as pltpu
from jax.sharding import Mesh, PartitionSpec as P

CAP = 6
PAD = 8
BF16 = jnp.bfloat16
F32 = jnp.float32
VMEM_LIMIT = 32 * 1024 * 1024
SMALL_LIMIT = 32 * 1024 * 1024
BIG_LIMIT = 60 * 1024 * 1024


def dot(a, b, ca=1, cb=0):
    return lax.dot_general(a, b, (((ca,), (cb,)), ((), ())), preferred_element_type=F32)


def whole():
    return pl.BlockSpec(memory_space=pltpu.VMEM)


def hbm():
    return pl.BlockSpec(memory_space=pltpu.HBM)


def start(pairs, sems):
    copies = [pltpu.make_async_copy(src, dst, sems.at[i]) for i, (src, dst) in enumerate(pairs)]
    for one in copies:
        one.start()
    return copies


def smem():
    return pl.BlockSpec(memory_space=pltpu.SMEM)


def tail_slot(row, q):
    return jnp.where(row == 6, q, jnp.where(row == 7, 3 + q, -1))


def main_slot(row):
    return jnp.where(row < CAP, row, -1)


def prep_kernel(core_ref, routes_ref, weight_ref, tok_ref, go_ref, out_ref, sel_ref, wsel_ref, scale_s):
    picks, rows = routes_ref.shape
    lanes = sel_ref.shape[1]
    half = tok_ref.shape[1] // 2

    @pl.when(pl.program_id(0) == 0)
    def _():
        slot = lax.broadcasted_iota(jnp.int32, (lanes, rows), 0)
        expert, row = slot >> 3, slot & 7
        named = jnp.zeros((lanes, rows), F32)
        weight = jnp.zeros((lanes, rows), F32)
        for k in range(picks):
            hit = routes_ref[k : k + 1, :] == expert
            named = named + jnp.where(hit, 1.0, 0.0)
            weight = weight + jnp.where(hit, weight_ref[k : k + 1, :], 0.0)
        earlier = lax.broadcasted_iota(jnp.int32, (rows, rows), 0) < lax.broadcasted_iota(jnp.int32, (rows, rows), 1)
        before = dot(named.astype(BF16), jnp.where(earlier, 1.0, 0.0).astype(BF16))
        picked, scales = [], []
        for i, want in enumerate([main_slot(row)] + [tail_slot(row, q) for q in range(3)]):
            one = jnp.where((named > 0.5) & (before == want.astype(F32)), 1.0, 0.0)
            sel_ref[i] = one.astype(BF16)
            picked.append(one)
            scales.append(jnp.sum(one * weight, axis=1, keepdims=True))
        plain = jnp.where((lax.broadcasted_iota(jnp.int32, (lanes, 1), 0) & 7) < CAP, 1.0, 0.0)
        scale_s[0] = plain + scales[1]
        scale_s[1] = plain + scales[2]
        scale_s[2] = scales[0] + scales[3]
        wsel = picked[0] * weight
        high = wsel.astype(BF16)
        wsel_ref[0] = high
        wsel_ref[1] = (wsel - high.astype(F32)).astype(BF16)

    own = pl.multiple_of(core_ref[0] * half, 128)
    other = pl.multiple_of((1 - core_ref[0]) * half, 128)
    tail = go_ref[:, pl.ds(other, half)]
    sources = (tok_ref[:, pl.ds(own, half)], tok_ref[:, pl.ds(other, half)], go_ref[:, pl.ds(own, half)])
    tails = dot(sel_ref[1:].reshape(3 * sel_ref.shape[1], sel_ref.shape[2]), tail)
    for q, source in enumerate(sources):
        rows_q = dot(sel_ref[0], source) + tails[q * sel_ref.shape[1] : (q + 1) * sel_ref.shape[1]]
        out_ref[0, :, q * half : (q + 1) * half] = (scale_s[q] * rows_q).astype(BF16)


def prep(core, routes, route_weight, tokens, grad_out, quarters, experts):
    rows, width = tokens.shape
    lanes = experts * PAD
    quarter = width // quarters
    half = quarter // 2
    column = pl.BlockSpec((rows, quarter), lambda i: (0, i))
    return pl.pallas_call(
        prep_kernel,
        grid=(quarters,),
        in_specs=[smem(), whole(), whole(), column, column],
        out_specs=[
            pl.BlockSpec((1, lanes, 3 * half), lambda i: (i, 0, 0)),
            pl.BlockSpec((4, lanes, rows), lambda i: (0, 0, 0)),
            pl.BlockSpec((2, lanes, rows), lambda i: (0, 0, 0)),
        ],
        out_shape=[
            jax.ShapeDtypeStruct((quarters, lanes, 3 * half), BF16),
            jax.ShapeDtypeStruct((4, lanes, rows), BF16),
            jax.ShapeDtypeStruct((2, lanes, rows), BF16),
        ],
        scratch_shapes=[pltpu.VMEM((3, lanes, 1), F32)],
        compiler_params=pltpu.CompilerParams(vmem_limit_bytes=BIG_LIMIT),
        cost_estimate=pl.CostEstimate(flops=800_000_000, bytes_accessed=6_500_000, transcendentals=0),
        name="prep",
    )(core, routes, route_weight, tokens, grad_out)


def slot_masks(slots, lanes, transposed=False):
    shape = (lanes, slots) if transposed else (slots, lanes)
    slot_dim, lane_dim = (1, 0) if transposed else (0, 1)
    slot = lax.broadcasted_iota(jnp.int32, shape, slot_dim)
    lane = lax.broadcasted_iota(jnp.int32, shape, lane_dim)
    expert = (slot * 171) >> 10
    place = slot - expert * CAP
    row = lane & 7
    same = (lane >> 3) == expert
    wants = [main_slot(row)] + [tail_slot(row, q) for q in range(3)]
    return [jnp.where(same & (place == want), 1.0, 0.0).astype(BF16) for want in wants]


def pair_of(ref, p, columns):
    return jnp.concatenate([ref[2 * p, :, columns], ref[2 * p + 1, :, columns]], axis=0)


def share_out(at_ref, total_s, outs):
    quarters = len(outs)
    slots = outs[0].shape[0]
    for j, out in enumerate(outs):
        rows = pl.ds(pl.multiple_of(lax.rem(at_ref[0] + j, quarters) * slots, 32), slots)
        out[...] = total_s[rows, :].astype(out.dtype)


def unpack_kernel(recv_any, wx_ref, own_ref, other_ref, total_ref, _, recv_s, sems):
    quarters, lanes, _ = recv_any.shape
    half = own_ref.shape[1]
    slots = own_ref.shape[0] // quarters
    pairs = quarters // 2
    copies = start([(recv_any.at[pl.ds(2 * p, 2), :, pl.ds(0, 2 * half)], recv_s.at[p]) for p in range(pairs)], sems)
    main = slot_masks(2 * slots, 2 * lanes)[0]
    for p in range(pairs):
        rows = slice(2 * p * slots, 2 * (p + 1) * slots)
        copies[p].wait()
        block = jnp.concatenate([recv_s[p, 0], recv_s[p, 1]], axis=0)
        own_ref[rows, :] = dot(main, block[:, :half]).astype(BF16)
        other_ref[rows, :] = dot(main, block[:, half:]).astype(BF16)
    total_ref[...] = dot(other_ref[...], wx_ref[...])


def unpack_x(recv, other_weight, slots):
    quarters, lanes, _ = recv.shape
    half, hidden = other_weight.shape
    anywhere = pl.BlockSpec(memory_space=pl.ANY)
    rows = jax.ShapeDtypeStruct((quarters * slots, half), BF16)
    return pl.pallas_call(
        unpack_kernel,
        in_specs=[anywhere, whole()],
        out_specs=[whole()] * 3 + [anywhere],
        out_shape=[
            rows,
            rows,
            jax.ShapeDtypeStruct((quarters * slots, hidden), F32),
            jax.ShapeDtypeStruct(recv.shape, BF16),
        ],
        scratch_shapes=[
            pltpu.VMEM((quarters // 2, 2, lanes, 2 * half), BF16),
            pltpu.SemaphoreType.DMA((quarters // 2,)),
        ],
        input_output_aliases={0: 3},
        compiler_params=pltpu.CompilerParams(vmem_limit_bytes=VMEM_LIMIT),
        cost_estimate=pl.CostEstimate(flops=2_000_000_000, bytes_accessed=6_000_000, transcendentals=0),
        name="unpack_x",
    )(recv, other_weight)


def gate_kernel(at_ref, own_ref, part_ref, wo_ref, p0_ref, p1_ref, p2_ref, p3_ref, total_s):
    total_s[...] = part_ref[...] + dot(own_ref[...], wo_ref[...])
    share_out(at_ref, total_s, (p0_ref, p1_ref, p2_ref, p3_ref))


def up_kernel(at_ref, own_ref, other_ref, wo_ref, wx_ref, p0_ref, p1_ref, p2_ref, p3_ref, total_s):
    total_s[...] = dot(own_ref[...], wo_ref[...]) + dot(other_ref[...], wx_ref[...])
    share_out(at_ref, total_s, (p0_ref, p1_ref, p2_ref, p3_ref))


def back_kernel(at_ref, recv_ref, wo_ref, wx_ref, p0_ref, p1_ref, p2_ref, p3_ref, own_ref, other_ref, total_s):
    quarters, lanes, _ = recv_ref.shape
    half = wo_ref.shape[1]
    slots = p0_ref.shape[0]
    masks = slot_masks(2 * slots, 2 * lanes)
    for p in range(quarters // 2):
        rows = slice(2 * p * slots, 2 * (p + 1) * slots)
        blocks = [pair_of(recv_ref, p, slice(q * half, (q + 1) * half)) for q in range(3)]
        own_ref[rows, :] = dot(masks[0], blocks[2]).astype(BF16)
        other_ref[rows, :] = sum(dot(masks[1 + q], blocks[q]) for q in range(3)).astype(BF16)
    total_s[...] = dot(own_ref[...], wo_ref[...], 1, 1) + dot(other_ref[...], wx_ref[...], 1, 1)
    share_out(at_ref, total_s, (p0_ref, p1_ref, p2_ref, p3_ref))


def projection(kernel, name, at, rows, weights, over, slots, quarters):
    half, hidden = weights[0].shape[over], weights[0].shape[1 - over]
    outs = [jax.ShapeDtypeStruct((slots, hidden), F32 if j == 0 else BF16) for j in range(quarters)]
    if len(rows) == 1:
        outs = outs + [jax.ShapeDtypeStruct((quarters * slots, half), BF16)] * 2
    return pl.pallas_call(
        kernel,
        in_specs=[smem()] + [whole()] * (len(rows) + len(weights)),
        out_specs=[whole()] * len(outs),
        out_shape=outs,
        scratch_shapes=[pltpu.VMEM((quarters * slots, hidden), F32)],
        compiler_params=pltpu.CompilerParams(vmem_limit_bytes=VMEM_LIMIT),
        cost_estimate=pl.CostEstimate(flops=3_000_000_000, bytes_accessed=8_000_000, transcendentals=0),
        name=name,
    )(at, *rows, *weights)


def gather_parts(at_ref, parts, all_s):
    quarters = len(parts)
    slots = parts[0].shape[0]
    for j, part in enumerate(parts):
        rows = pl.ds(pl.multiple_of(lax.rem(at_ref[0] + j, quarters) * slots, 32), slots)
        all_s[rows, :] = part[...]


def out_kernel(at_ref, h0, h1, h2, h3, wo_ref, wx_ref, out_ref, all_ref):
    quarters, lanes, width = out_ref.shape
    half = width // 2
    slots = h0.shape[0]
    gather_parts(at_ref, (h0, h1, h2, h3), all_ref)
    main = slot_masks(2 * slots, 2 * lanes, True)[0]
    for q, w_ref in enumerate((wo_ref, wx_ref)):
        value = dot(all_ref[...], w_ref[...]).astype(BF16)
        for p in range(quarters // 2):
            rows = dot(main, value[2 * p * slots : 2 * (p + 1) * slots]).astype(BF16)
            out_ref[2 * p, :, q * half : (q + 1) * half] = rows[:lanes]
            out_ref[2 * p + 1, :, q * half : (q + 1) * half] = rows[lanes:]


def out_rows(at, parts, weights, lanes):
    quarters = len(parts)
    slots, hidden = parts[0].shape
    half = weights[0].shape[1]
    return pl.pallas_call(
        out_kernel,
        in_specs=[smem()] + [whole()] * (quarters + 2),
        out_specs=[whole()] * 2,
        out_shape=[
            jax.ShapeDtypeStruct((quarters, lanes, 2 * half), BF16),
            jax.ShapeDtypeStruct((quarters * slots, hidden), BF16),
        ],
        compiler_params=pltpu.CompilerParams(vmem_limit_bytes=VMEM_LIMIT),
        cost_estimate=pl.CostEstimate(flops=2_000_000_000, bytes_accessed=7_500_000, transcendentals=0),
        name="out_rows",
    )(at, *parts, *weights)


def half_grad_kernel(at_ref, g0, g1, g2, g3, wo_ref, wx_ref, own_ref, other_ref, keep_hbm, all_s, sem):
    gather_parts(at_ref, (g0, g1, g2, g3), all_s)
    keep = pltpu.make_async_copy(all_s, keep_hbm, sem)
    keep.start()
    own_ref[...] = dot(all_s[...], wo_ref[...], 1, 1)
    other_ref[...] = dot(all_s[...], wx_ref[...], 1, 1)
    keep.wait()


def half_grad(at, parts, weights):
    quarters = len(parts)
    slots, hidden = parts[0].shape
    value = jax.ShapeDtypeStruct((quarters * slots, weights[0].shape[0]), F32)
    return pl.pallas_call(
        half_grad_kernel,
        in_specs=[smem()] + [whole()] * (quarters + 2),
        out_specs=[whole(), whole(), hbm()],
        out_shape=[value, value, jax.ShapeDtypeStruct((quarters * slots, hidden), BF16)],
        scratch_shapes=[pltpu.VMEM((quarters * slots, hidden), BF16), pltpu.SemaphoreType.DMA],
        compiler_params=pltpu.CompilerParams(vmem_limit_bytes=SMALL_LIMIT),
        cost_estimate=pl.CostEstimate(flops=1_500_000_000, bytes_accessed=8_000_000, transcendentals=0),
        name="half_grad",
    )(at, *parts, *weights)


def grad_kernel(at_ref, g0, g1, g2, g3, main_ref, half_own_ref, half_other_ref, wo_hbm, wx_hbm, out_ref, keep_hbm, all_s, w_s, sem, load_sems):
    loads = start([(wx_hbm, w_s.at[0]), (wo_hbm, w_s.at[1])], load_sems)
    quarters, lanes, packed = out_ref.shape
    half = packed // 3
    slots = g0.shape[0]
    gather_parts(at_ref, (g0, g1, g2, g3), all_s)
    keep = pltpu.make_async_copy(all_s, keep_hbm, sem)
    keep.start()
    masks = slot_masks(2 * slots, 2 * lanes, True)
    tail_masks = jnp.concatenate(masks[1:], axis=0)
    loads[0].wait()
    other = (half_other_ref[...] + dot(all_s[...], w_s[0], 1, 1)).astype(BF16)
    loads[1].wait()
    own = (half_own_ref[...] + dot(all_s[...], w_s[1], 1, 1)).astype(BF16)
    for p in range(quarters // 2):
        rows = slice(2 * p * slots, 2 * (p + 1) * slots)
        tails = dot(tail_masks, other[rows])
        for q in range(3):
            columns = slice(q * half, (q + 1) * half)
            value = tails[2 * q * lanes : 2 * (q + 1) * lanes]
            if q == 2:
                value = value + dot(masks[0], own[rows])
            for i in range(2):
                part = value[i * lanes : (i + 1) * lanes].astype(BF16)
                out_ref[2 * p + i, :, columns] = part if q == 2 else part + main_ref[2 * p + i, :, columns]
    keep.wait()


def grad_rows(at, parts, main, halves, weights):
    quarters, lanes, width = main.shape
    slots, hidden = parts[0].shape
    return pl.pallas_call(
        grad_kernel,
        in_specs=[smem()] + [whole()] * (quarters + 3) + [hbm()] * 2,
        out_specs=[whole(), hbm()],
        out_shape=[
            jax.ShapeDtypeStruct((quarters, lanes, width // 2 * 3), BF16),
            jax.ShapeDtypeStruct((quarters * slots, hidden), BF16),
        ],
        scratch_shapes=[
            pltpu.VMEM((quarters * slots, hidden), BF16),
            pltpu.VMEM((2, *weights[0].shape), BF16),
            pltpu.SemaphoreType.DMA,
            pltpu.SemaphoreType.DMA((2,)),
        ],
        compiler_params=pltpu.CompilerParams(vmem_limit_bytes=SMALL_LIMIT),
        cost_estimate=pl.CostEstimate(flops=2_500_000_000, bytes_accessed=14_000_000, transcendentals=0),
        name="grad_rows",
    )(at, *parts, main, *halves, *weights)


def weight_kernel(am_ref, ap_ref, bm_ref, bp_ref, out_ref):
    out_ref[...] = (dot(am_ref[...], bm_ref[...], 0, 0) + dot(ap_ref[...], bp_ref[...], 0, 0)).astype(BF16)


def weight_grad(a_mine, a_partner, b_mine, b_partner, step, at=0, columns=None):
    slots, rows = a_mine.shape
    columns = columns or b_mine.shape[1]
    a_spec = pl.BlockSpec((slots, rows), lambda n: (0, 0))
    b_spec = pl.BlockSpec((slots, step), lambda n: (0, n + at))
    return pl.pallas_call(
        weight_kernel,
        grid=(columns // step,),
        in_specs=[a_spec, a_spec, b_spec, b_spec],
        out_specs=pl.BlockSpec((rows, step), lambda n: (0, n)),
        out_shape=jax.ShapeDtypeStruct((rows, columns), BF16),
        compiler_params=pltpu.CompilerParams(vmem_limit_bytes=VMEM_LIMIT),
        cost_estimate=pl.CostEstimate(flops=1_500_000_000, bytes_accessed=5_000_000, transcendentals=0),
        name="weight_grad",
    )(a_mine, a_partner, b_mine, b_partner)


def last_kernel(core_ref, routes_ref, sel_ref, wsel_ref, recv_ref, go_ref, moe_ref, gt_ref, gr_ref, inner_s, lhs_s):
    step = pl.program_id(0)
    half = go_ref.shape[1] // 2
    own = pl.ds(pl.multiple_of(core_ref[0] * half, 128), half)
    other = pl.ds(pl.multiple_of((1 - core_ref[0]) * half, 128), half)
    block = [recv_ref[0, :, q * half : (q + 1) * half] for q in range(3)]
    rows = go_ref.shape[0]

    @pl.when(step == 0)
    def _():
        for q in range(2):
            for i, one in enumerate((wsel_ref[0], wsel_ref[1], sel_ref[1 + q])):
                lhs_s[q, i * rows : (i + 1) * rows, :] = one.astype(F32).T.astype(BF16)
        for i in (0, 3):
            lhs_s[2, i // 3 * rows : (i // 3 + 1) * rows, :] = sel_ref[i].astype(F32).T.astype(BF16)

    first, second, third = dot(lhs_s[0], block[0]), dot(lhs_s[1], block[1]), dot(lhs_s[2, : 2 * rows, :], block[2])
    moe_ref[:, own] = (first[:rows] + first[rows : 2 * rows]).astype(BF16)
    moe_ref[:, other] = (second[:rows] + second[rows : 2 * rows]).astype(BF16)
    gt_ref[:, own] = third[:rows].astype(BF16)
    gt_ref[:, other] = (first[2 * rows :] + second[2 * rows :] + third[rows:]).astype(BF16)
    inner = dot(block[0], go_ref[:, own], 1, 1) + dot(block[1], go_ref[:, other], 1, 1)

    @pl.when(step == 0)
    def _():
        inner_s[...] = inner

    @pl.when(step > 0)
    def _():
        inner_s[...] += inner

    @pl.when(step == pl.num_programs(0) - 1)
    def _():
        picks, rows = routes_ref.shape
        lanes = sel_ref.shape[1]
        expert = lax.broadcasted_iota(jnp.int32, (lanes, rows), 0) >> 3
        held = sel_ref[0].astype(F32) * inner_s[...]
        for k in range(picks):
            mine = jnp.where(routes_ref[k : k + 1, :] == expert, held, 0.0)
            gr_ref[k : k + 1, :] = jnp.sum(mine, axis=0, keepdims=True)


def last(core, routes, sel, wsel, recv, grad_out):
    rows, width = grad_out.shape
    quarters, lanes, packed = recv.shape
    column = pl.BlockSpec((rows, width // quarters), lambda i: (0, i))
    return pl.pallas_call(
        last_kernel,
        grid=(quarters,),
        in_specs=[smem(), whole(), whole(), whole(), pl.BlockSpec((1, lanes, packed), lambda i: (i, 0, 0)), column],
        out_specs=[column, column, pl.BlockSpec(routes.shape, lambda i: (0, 0))],
        out_shape=[
            jax.ShapeDtypeStruct((rows, width), BF16),
            jax.ShapeDtypeStruct((rows, width), BF16),
            jax.ShapeDtypeStruct(routes.shape, F32),
        ],
        scratch_shapes=[pltpu.VMEM((lanes, rows), F32), pltpu.VMEM((3, 3 * rows, lanes), BF16)],
        compiler_params=pltpu.CompilerParams(vmem_limit_bytes=BIG_LIMIT),
        cost_estimate=pl.CostEstimate(flops=1_500_000_000, bytes_accessed=8_500_000, transcendentals=0),
        name="last",
    )(core, routes, sel, wsel, recv, grad_out)


def on_device(tokens, routes, route_weight, w_gate, w_up, w_down, grad_out):
    quarters = lax.axis_size("y")
    experts = lax.axis_size("x") * lax.axis_size("z")
    slots = experts * CAP
    lanes = experts * PAD
    hidden = w_gate.shape[2]
    everyone = ("y", "x", "z")
    half = w_gate.shape[1]
    core = lax.axis_index("k").astype(jnp.int32).reshape(1)
    at = lax.axis_index("y").astype(jnp.int32).reshape(1)

    def to_partner(value):
        return lax.ppermute(value, "k", [(0, 1), (1, 0)])

    def along(value, shift):
        return lax.ppermute(value, "y", [(i, (i + shift) % quarters) for i in range(quarters)])

    def exchange(value):
        flat = value.reshape(quarters * experts, PAD, value.shape[2])
        return lax.all_to_all(flat, everyone, 0, 0, tiled=True).reshape(value.shape)

    def add_over_y(shares):
        total = shares[0]
        for j in (2, 1, 3):
            total = total + along(shares[j], j).astype(F32)
        return total

    def from_y(value):
        got = {j: along(value, quarters - j) for j in (2, 1, 3)}
        return [value, got[1], got[2], got[3]]

    gate_own, up_own, down_own = w_gate[0], w_up[0], w_down[0]
    gate_other, up_other, down_other = to_partner(gate_own), to_partner(up_own), to_partner(down_own)
    routes, route_weight = routes.T, route_weight.T

    sent, sel, wsel = prep(core, routes, route_weight, tokens, grad_out, quarters, experts)
    recv = exchange(sent)
    down = (down_own, down_other)
    x_own, x_other, part, recv = unpack_x(recv, gate_other, slots)
    gate = add_over_y(projection(gate_kernel, "gate", at, (x_own, part), (gate_own,), 0, slots, quarters))
    shares = projection(up_kernel, "up", at, (x_own, x_other), (up_own, up_other), 0, slots, quarters)
    up = add_over_y(shares)
    *shares, d_own, d_other = projection(back_kernel, "back", at, (recv,), down, 1, slots, quarters)
    back = add_over_y(shares)

    sig = jax.nn.sigmoid(gate)
    smooth = gate * sig
    slope = up * (sig * (1.0 + gate * (1.0 - sig)))
    mine, smooth, slope = lax.optimization_barrier(((smooth * up).astype(BF16), smooth, slope))
    h_parts = from_y(mine)
    back, h_parts = lax.optimization_barrier((back, h_parts))
    dg_parts = from_y((back * slope).astype(BF16))
    main, h_mine = out_rows(at, h_parts, down, lanes)
    du, main = lax.optimization_barrier(((back * smooth).astype(BF16), main))
    du_parts = from_y(du)
    *halves, dg_mine = half_grad(at, dg_parts, (gate_own, gate_other))
    packed, du_mine = grad_rows(at, du_parts, main, halves, (up_own, up_other))
    x_other, d_other, h_mine, dg_mine, du_mine = lax.optimization_barrier((x_other, d_other, h_mine, dg_mine, du_mine))
    returned = exchange(packed)

    x_partner, d_partner, h_partner = to_partner(x_other), to_partner(d_other), to_partner(h_mine)
    dg_partner, du_partner = to_partner(dg_mine), to_partner(du_mine)
    step = hidden // 4
    grad_down = weight_grad(h_mine, h_partner, d_own, d_partner, half)
    grad_gate = weight_grad(x_own, x_partner, dg_mine, dg_partner, step)
    grad_up = weight_grad(x_own, x_partner, du_mine, du_partner, step)
    returned, grad_gate, grad_up, grad_down = lax.optimization_barrier((returned, grad_gate, grad_up, grad_down))

    moe_out, grad_tokens, grad_route = last(core, routes, sel, wsel, returned, grad_out)
    return (moe_out, grad_tokens, grad_route.T, grad_gate[None], grad_up[None], grad_down[None])


def solution(mesh):
    ctx, head = mesh.shape["ctx"], mesh.shape["head"]
    side = int(round(ctx**0.5))
    fine = Mesh(mesh.devices.reshape(side, ctx // side, head // 2, 2), ("x", "z", "y", "k"))
    e, d, both = ("x", "z"), ("y", "k"), ("x", "z", "y", "k")
    rows = P(both, None)
    up, down = P(e, d, None), P(e, None, d)
    return jax.shard_map(
        on_device,
        mesh=fine,
        in_specs=(rows, rows, rows, up, up, down, rows),
        out_specs=(rows, rows, rows, up, up, down),
        check_vma=False,
    )
```
